256 devices in a mesh: slab: 32 (over y, x, core), led: 8 (over z).
Axes of the slice: x: 4, y: 4, z: 8, core: 2. Of those that a mesh axis runs over, the one named last changes fastest.
Arguments:
- spectrum: float32 [2, 4096, 3072], P(None, 'slab'), may hold values from -6 to 6
- pupil: float32 [2, 2048, 2048], P(None, 'slab'), may hold values from -6 to 6
- intensity: float32 [8, 2048, 2048], P('led', 'slab'), may hold values from 0.1 to 4
- row_offsets: int32 [8], replicated, may hold values from 0 to 2048, as said below
- col_offsets: int32 [8], replicated, may hold values from 0 to 1024, as said below
Outputs:
- new_spectrum: float32 [2, 4096, 3072], P(None, 'slab')
- pupil_grad: float32 [2, 2048, 2048], P(None, 'slab')
The draws below stay inside these ranges and needn't reach their ends.
Inputs may be any that keep to these rules, and one draw needn't show every extreme that they name: `row_offsets`: every LED's subaperture lies inside the spectrum; some LED starts at row 0 and some at row 2048. `col_offsets`: every LED's subaperture lies inside the spectrum; some LED starts at column 0 and some at column 1024.
All inputs are finite; a program needn't handle non-finite values.
Results may differ from the reference program's by a relative error of at most 0.012.
The reference program's roundings to bfloat16 on the way count: a program that leaves them out, or rounds other values in their place, can miss the bound.
Values may be sent and summed in bfloat16 or wider, within the bound.
No kernel may reach another device: no remote copies, remote signals or barrier semaphores. Data moves between devices by JAX's collectives and lax.ppermute only.
A program may use at most 64 MiB of HBM per device.

```python
import math
import jax
import jax.numpy as jnp
from jax import lax

W = 2048
NR = 4096
NC = 3072
LEDS = 8


def offsets_with_ends(key, count, highest):
    first_key, second_key = jax.random.split(key)
    values = jax.random.randint(first_key, (count,), 0, highest + 1, dtype=jnp.int32)
    order = jax.random.permutation(second_key, count)
    values = values.at[order[0]].set(0)
    values = values.at[order[1]].set(highest)
    return values


def draw_row_offsets(key, part):
    key = jax.random.fold_in(key, 11)
    return offsets_with_ends(key, LEDS, NR - W)


def draw_col_offsets(key, part):
    key = jax.random.fold_in(key, 12)
    return offsets_with_ends(key, LEDS, NC - W)


def shard_levels(key, extent, cuts, low, top_value):
    loudness, own = 1.0, jax.random.fold_in(key, 6)
    for axis_at, parts in cuts:
        steps = jnp.exp(jax.random.uniform(jax.random.fold_in(own, axis_at), (parts,), jnp.float32, low / len(cuts), top_value / len(cuts)))
        loudness = loudness * jnp.repeat(steps, extent[axis_at] // parts).reshape([-1 if axis == axis_at else 1 for axis in range(len(extent))])
    return loudness


def noise(own_key, extent, spread, most, cuts=(), kind=jnp.bfloat16):
    gain = shard_levels(own_key, extent, cuts, -0.22, 0.18) if cuts else 1.0
    result = jax.random.normal(own_key, extent, jnp.float32) * spread * gain
    return jnp.minimum(jnp.maximum(result, -most), most).astype(kind)


def setup_inputs(seed: int = 0) -> dict:
    arg_keys = jax.random.split(jax.random.key(seed), 6)
    spectrum = noise(arg_keys[0], (2, NR, NC), 1.0, 6.0, ((1, 32),), jnp.float32)
    pupil = noise(arg_keys[1], (2, W, W), 1.0, 6.0, ((1, 32),), jnp.float32)
    intensity = jnp.clip(0.1 + 3.9 * jax.random.uniform(arg_keys[2], (LEDS, W, W), jnp.float32) ** shard_levels(arg_keys[2], (LEDS, W, W), ((0, 8), (1, 32)), -0.2, 0.2), 0.1, 4.0)
    row_offsets = draw_row_offsets(jax.random.fold_in(arg_keys[5], 71), 0)
    col_offsets = draw_col_offsets(jax.random.fold_in(arg_keys[5], 71), 0)
    return {"spectrum": spectrum, "pupil": pupil, "intensity": intensity, "row_offsets": row_offsets, "col_offsets": col_offsets}


AMPLITUDE_FLOOR = 0.5
PUPIL_DAMPING = 0.5

def tables(length):
    counter = jnp.arange(length, dtype=jnp.int32)
    products = counter[:, None] * counter[None, :] % length
    phases = products.astype(jnp.float32) * (2.0 * math.pi / length)
    factor = 1.0 / math.sqrt(length)
    return ((jnp.cos(phases) * factor).astype(jnp.bfloat16), (jnp.sin(phases) * factor).astype(jnp.bfloat16))

def transform(values, cosine_table, sine_table, direction):
    height = values.shape[1]
    flattened = values.reshape(2 * height, values.shape[2])
    with_cos = jnp.dot(flattened, cosine_table, preferred_element_type=jnp.float32).reshape(2, height, -1)
    with_sin = jnp.dot(flattened, sine_table, preferred_element_type=jnp.float32).reshape(2, height, -1)
    real_part = with_cos[0] - direction * with_sin[1]
    imag_part = with_cos[1] + direction * with_sin[0]
    return jnp.stack([real_part, imag_part])

def reference(spectrum, pupil, intensity, row_offsets, col_offsets):
    cosine_table, sine_table = tables(W)
    pupil_weight = pupil[0] * pupil[0] + pupil[1] * pupil[1] + PUPIL_DAMPING

    def one_led(carry, inputs):
        gradient, update = carry
        measured, row_start, col_start = inputs
        anchor = jnp.zeros((), jnp.int32)
        region = lax.dynamic_slice(spectrum, (anchor, row_start, col_start), (2, W, W))
        rounded = lax.optimization_barrier(jnp.swapaxes(region, 1, 2).astype(jnp.bfloat16))
        window = rounded.astype(jnp.float32)
        prod_real = window[0] * pupil[0] - window[1] * pupil[1]
        prod_imag = window[0] * pupil[1] + window[1] * pupil[0]
        product = jnp.stack([prod_real, prod_imag])
        first_pass = transform(product.astype(jnp.bfloat16), cosine_table, sine_table, 1.0).astype(jnp.bfloat16)
        image_field = transform(jnp.swapaxes(first_pass, 1, 2), cosine_table, sine_table, 1.0)
        magnitude = jnp.sqrt(image_field[0] * image_field[0] + image_field[1] * image_field[1])
        scaling = jnp.sqrt(measured) / jnp.maximum(magnitude, AMPLITUDE_FLOOR)
        replaced = (image_field * scaling).astype(jnp.bfloat16)
        second_pass = transform(replaced, cosine_table, sine_table, -1.0).astype(jnp.bfloat16)
        estimate = transform(jnp.swapaxes(second_pass, 1, 2), cosine_table, sine_table, -1.0)
        change = estimate - product
        grad_real = window[0] * change[0] + window[1] * change[1]
        grad_imag = window[0] * change[1] - window[1] * change[0]
        gradient = gradient + jnp.stack([grad_real, grad_imag])
        corr_real = (pupil[0] * change[0] + pupil[1] * change[1]) / pupil_weight
        corr_imag = (pupil[0] * change[1] - pupil[1] * change[0]) / pupil_weight
        placed = jnp.swapaxes(jnp.stack([corr_real, corr_imag]), 1, 2)
        current = lax.dynamic_slice(update, (anchor, row_start, col_start), (2, W, W))
        update = lax.dynamic_update_slice(update, current + placed, (anchor, row_start, col_start))
        return ((gradient, update), None)
    start = (jnp.zeros((2, W, W), jnp.float32), jnp.zeros((2, NR, NC), jnp.float32))
    (gradient, update), ignored = lax.scan(one_led, start, (intensity, row_offsets, col_offsets))
    return (spectrum + update, gradient)
```

```python
import functools
import math

import jax
import jax.numpy as jnp
import numpy as np
from jax import lax
from jax.experimental import pallas as pl
from jax.experimental.pallas import tpu as pltpu
from jax.sharding import PartitionSpec as P

W = 2048
QUARTER = W // 4
BAND = 64
NC = 3072
AMPLITUDE_FLOOR = 0.5
PUPIL_DAMPING = 0.5
MIB = 1024 * 1024

VMEM = pltpu.VMEM
F32 = jnp.float32
BF16 = jnp.bfloat16


def table():
    rows = np.arange(QUARTER, dtype=np.int64)[:, None]
    cols = np.arange(W, dtype=np.int64)[None, :]
    phases = ((rows * cols) % W).astype(np.float32) * np.float32(2.0 * math.pi / W)
    factor = np.float32(1.0 / math.sqrt(W))
    parts = []
    for res in range(4):
        part = phases[:, res::4]
        parts.append(np.concatenate([np.cos(part) * factor, np.sin(part) * factor], 1))
    return np.stack(parts).astype(jnp.bfloat16)


def low_half(shape):
    return lax.broadcasted_iota(jnp.int32, shape, 1) < BAND


def swap(x):
    return pltpu.roll(x, BAND, 1)


def times_i(x):
    s = swap(x)
    return jnp.where(low_half(x.shape), -s, s)


def dft(x_ref, t_ref, g_ref, sign, emit):
    for res in range(4):
        x = x_ref[pl.ds(res, QUARTER, stride=4), :]
        ix = times_i(x)
        if sign < 0:
            ix = -ix
        operand = jnp.concatenate([x.astype(BF16), ix.astype(BF16)], 0)
        g_ref[res] = jnp.dot(t_ref[res], operand, preferred_element_type=F32)

    def combine(step, carry):
        rows = pl.ds(pl.multiple_of(step * 128, 128), 128)
        g0, g1, g2, g3 = g_ref[0, rows, :], g_ref[1, rows, :], g_ref[2, rows, :], g_ref[3, rows, :]
        h0, h1, h2 = g0 + g2, g0 - g2, g1 + g3
        h3 = times_i(g1 - g3)
        if sign < 0:
            h3 = -h3
        emit(0, step, h0 + h2)
        emit(1, step, h1 + h3)
        emit(2, step, h0 - h2)
        emit(3, step, h1 - h3)
        return carry

    lax.fori_loop(0, QUARTER // 128, combine, 0)


def emit_turned(out_ref):
    def emit(r, step, value):
        turned = value.T
        a, b = turned[:BAND], turned[BAND:]
        low = low_half(a.shape)
        first = jnp.where(low, a, swap(b)).astype(BF16)
        second = jnp.where(low, swap(a), b).astype(BF16)
        base = pl.multiple_of(r * QUARTER + step * 128, 128)
        out_ref[pl.ds(base, BAND), :] = first
        out_ref[pl.ds(pl.multiple_of(base + BAND, BAND), BAND), :] = second

    return emit


def gather_kernel(off_ref, spec_ref, out_ref):
    col = off_ref[1]
    tile = col // 128
    lo = col - tile * 128
    shift = lax.rem(128 - lo, 128)
    lanes = lax.broadcasted_iota(jnp.int32, (128, 128), 1)
    keep = lanes < 128 - lo
    low = lanes < BAND

    def load(k, t):
        t = jnp.minimum(tile + t, NC // 128 - 1)
        x = spec_ref[k, :, pl.ds(pl.multiple_of(t * 128, 128), 128)]
        return pltpu.roll(x, shift, 1)

    def step(t, carry):
        nxt = (load(0, t + 1), load(1, t + 1))
        a = jnp.where(keep, carry[0], nxt[0])
        b = jnp.where(keep, carry[1], nxt[1])
        base = pl.multiple_of(t * 256, 256)
        out_ref[pl.ds(base, 128), :] = jnp.where(low, a, swap(b)).astype(BF16)
        out_ref[pl.ds(pl.multiple_of(base + 128, 128), 128), :] = jnp.where(low, swap(a), b).astype(BF16)
        return nxt

    lax.fori_loop(0, W // 128, step, (load(0, 0), load(1, 0)))


def prepare_kernel(pupil_ref, intensity_ref, pr_ref, pi_ref, root_ref):
    def step(t, carry):
        rows = pl.ds(pl.multiple_of(t * 128, 128), 128)
        x = jnp.concatenate([pupil_ref[0, :, rows], pupil_ref[1, :, rows]], 0).T
        s = swap(x)
        low = low_half(x.shape)
        pr_ref[rows, :] = jnp.where(low, x, s)
        pi_ref[rows, :] = jnp.where(low, -s, x)
        v = jnp.sqrt(intensity_ref[0, :, rows])
        root_ref[rows, :] = jnp.concatenate([v, v], 0).T
        return carry

    lax.fori_loop(0, W // 128, step, 0)


def first_kernel(off_ref, recv_ref, pr_ref, pi_ref, t_ref, out_ref, win_ref, wide_ref, x_ref, g_ref):
    row = off_ref[0]
    base = jnp.minimum(row // 16 * 16, 2 * W - (W + 16))
    off = row - base

    def widen(step, carry):
        src = pl.ds(pl.multiple_of(base + step * 48, 16), 48)
        wide_ref[pl.ds(pl.multiple_of(step * 48, 16), 48), :] = recv_ref[src, :].astype(F32)
        return carry

    lax.fori_loop(0, (W + 16) // 48, widen, 0)

    def multiply(step, carry):
        rows = pl.ds(pl.multiple_of(step * 128, 128), 128)
        w = wide_ref[pl.ds(off + step * 128, 128), :]
        product = w * pr_ref[rows, :] + swap(w) * pi_ref[rows, :]
        win_ref[rows, :] = w.astype(BF16)
        x_ref[rows, :] = product.astype(BF16).astype(F32)
        return carry

    lax.fori_loop(0, W // 128, multiply, 0)
    dft(x_ref, t_ref, g_ref, 1, emit_turned(out_ref))


def widen_rows(recv_ref, x_ref):
    def widen(step, carry):
        rows = pl.ds(pl.multiple_of(step * 128, 128), 128)
        x_ref[rows, :] = recv_ref[rows, :].astype(F32)
        return carry

    lax.fori_loop(0, W // 128, widen, 0)


def middle_kernel(recv_ref, root_ref, t_ref, out_ref, x_ref, y_ref, g_ref):
    widen_rows(recv_ref, x_ref)

    def replace(r, step, value):
        squared = value * value
        magnitude = jnp.sqrt(squared + swap(squared))
        rows = pl.ds(pl.multiple_of(r * QUARTER + step * 128, 128), 128)
        scaling = root_ref[rows, :] / jnp.maximum(magnitude, AMPLITUDE_FLOOR)
        y_ref[rows, :] = (value * scaling).astype(BF16).astype(F32)

    dft(x_ref, t_ref, g_ref, 1, replace)
    dft(y_ref, t_ref, g_ref, -1, emit_turned(out_ref))


def last_kernel(off_ref, recv_ref, win_ref, pr_ref, pi_ref, t_ref, grad_ref, corr_ref, x_ref, c_ref, g_ref):
    row = off_ref[0]
    widen_rows(recv_ref, x_ref)

    def update(r, step, estimate):
        start = r * QUARTER + step * 128
        rows = pl.ds(pl.multiple_of(start, 128), 128)
        w = win_ref[rows, :].astype(F32)
        pr, pi = pr_ref[rows, :], pi_ref[rows, :]
        ws = swap(w)
        low = low_half(w.shape)
        change = estimate - (w * pr + ws * pi)
        cs = swap(change)
        wr = jnp.where(low, w, ws)
        wi = jnp.where(low, ws, -w)
        grad_ref[rows, :] = (change * wr + cs * wi).astype(BF16)
        c_ref[pl.ds(row + start, 128), :] = (change * pr - cs * pi) / (pr * pr + pi * pi + PUPIL_DAMPING)

    c_ref[...] = jnp.zeros_like(c_ref)
    dft(x_ref, t_ref, g_ref, -1, update)

    def store(step, carry):
        rows = pl.ds(pl.multiple_of(step * 128, 128), 128)
        corr_ref[rows, :] = c_ref[rows, :].astype(BF16)
        return carry

    lax.fori_loop(0, 2 * W // 128, store, 0)


def place_kernel(off_ref, recv_ref, out_ref):
    col = off_ref[1]
    tile = col // 128
    lo = col - tile * 128
    lanes = lax.broadcasted_iota(jnp.int32, (128, 128), 1)
    low = lanes < BAND
    take = lanes >= lo
    out_ref[...] = jnp.zeros_like(out_ref)

    def put(k, t, value):
        t = jnp.minimum(tile + t, NC // 128 - 1)
        out_ref[k, :, pl.ds(pl.multiple_of(t * 128, 128), 128)] = value.astype(BF16)

    def step(t, carry):
        base = pl.multiple_of(t * 256, 256)
        x = recv_ref[pl.ds(base, 128), :].astype(F32)
        y = recv_ref[pl.ds(pl.multiple_of(base + 128, 128), 128), :].astype(F32)
        a = pltpu.roll(jnp.where(low, x, swap(y)), lo, 1)
        b = pltpu.roll(jnp.where(low, swap(x), y), lo, 1)
        put(0, t, jnp.where(take, a, carry[0]))
        put(1, t, jnp.where(take, b, carry[1]))
        return a, b

    zero = jnp.zeros((128, 128), F32)
    a, b = lax.fori_loop(0, W // 128, step, (zero, zero))

    @pl.when(lo > 0)
    def _():
        put(0, W // 128, jnp.where(take, 0.0, a))
        put(1, W // 128, jnp.where(take, 0.0, b))


def finish_kernel(spec_ref, update_ref, grad_ref, new_ref, out_ref):
    for k in range(2):
        def add(step, carry):
            rows = pl.ds(pl.multiple_of(step * 16, 16), 16)
            new_ref[k, rows, :] = spec_ref[k, rows, :] + update_ref[k, rows, :].astype(F32)
            return carry

        lax.fori_loop(0, 8, add, 0)

    def turn(t, carry):
        rows = pl.ds(pl.multiple_of(t * 128, 128), 128)
        x = grad_ref[rows, :].astype(F32).T
        out_ref[0, :, rows] = x[:BAND]
        out_ref[1, :, rows] = x[BAND:]
        return carry

    lax.fori_loop(0, W // 128, turn, 0)


def call(kernel, outs, scalars, arrays, scratch=(), flops=0):
    shapes = [jax.ShapeDtypeStruct(s, d) for s, d in outs]
    moved = sum(math.prod(s) * jnp.dtype(d).itemsize for s, d in outs)
    moved += sum(a.size * a.dtype.itemsize for a in arrays)
    return pl.pallas_call(
        kernel,
        out_shape=shapes,
        in_specs=[pl.BlockSpec(memory_space=pltpu.SMEM)] * len(scalars)
        + [pl.BlockSpec(memory_space=VMEM)] * len(arrays),
        out_specs=[pl.BlockSpec(memory_space=VMEM)] * len(outs),
        scratch_shapes=list(scratch),
        compiler_params=pltpu.CompilerParams(vmem_limit_bytes=40 * MIB),
        cost_estimate=pl.CostEstimate(flops=flops, bytes_accessed=moved, transcendentals=0),
    )(*scalars, *arrays)


def turn_bands(values):
    blocks = values.reshape(32, -1, 128)
    return lax.all_to_all(blocks, "slab", 0, 0).reshape(-1, 128)


def ring_gather(piece):
    forward = backward = piece
    found = [(0, piece)]
    for hop in range(1, 5):
        forward = lax.ppermute(forward, "led", [(i, (i + 1) % 8) for i in range(8)])
        found.append((hop, forward))
        if hop < 4:
            backward = lax.ppermute(backward, "led", [(i, (i - 1) % 8) for i in range(8)])
            found.append((-hop, backward))
    me = lax.axis_index("led")
    out = jnp.zeros((8,) + piece.shape, piece.dtype)
    for hop, value in found:
        out = lax.dynamic_update_index_in_dim(out, value, (me - hop) % 8, 0)
    return out


def per_device(spectrum, pupil, intensity, row_offsets, col_offsets):
    led = lax.axis_index("led")
    offsets = jnp.stack([row_offsets[led], col_offsets[led]])
    tab = jnp.asarray(table())
    rows128 = (W, 128)
    flops = 8 * QUARTER * 1024 * 128

    (outgoing,) = call(gather_kernel, [((2 * W, 128), BF16)], [offsets], [spectrum])
    arrived = turn_bands(outgoing)
    pr, pi, root = call(prepare_kernel, [(rows128, F32)] * 3, [], [pupil, intensity])
    scratch = [VMEM(rows128, F32), VMEM((4, QUARTER, 128), F32)]
    first, window = call(
        first_kernel,
        [(rows128, BF16), (rows128, BF16)],
        [offsets],
        [arrived, pr, pi, tab],
        [VMEM((W + 16, 128), F32)] + scratch,
        flops,
    )
    turned = turn_bands(first)
    (second,) = call(
        middle_kernel, [(rows128, BF16)], [], [turned, root, tab], [VMEM(rows128, F32)] + scratch, 2 * flops
    )
    returned = turn_bands(second)
    gradient, correction = call(
        last_kernel,
        [(rows128, BF16), ((2 * W, 128), BF16)],
        [offsets],
        [returned, window, pr, pi, tab],
        [VMEM(rows128, F32), VMEM((2 * W, 128), F32), VMEM((4, QUARTER, 128), F32)],
        flops,
    )
    grad_part = lax.psum_scatter(gradient.reshape(8, W // 8, 128), "led", scatter_dimension=0)
    landed = turn_bands(correction)
    (placed,) = call(place_kernel, [((2, 128, NC), BF16)], [offsets], [landed])
    update_part = lax.psum_scatter(placed.reshape(2, 8, 16, NC), "led", scatter_dimension=1)
    grad_total = ring_gather(grad_part).reshape(rows128)
    update_total = jnp.swapaxes(ring_gather(update_part), 0, 1).reshape(2, 128, NC)
    new_spectrum, grad = call(
        finish_kernel,
        [((2, 128, NC), F32), ((2, BAND, W), F32)],
        [],
        [spectrum, update_total, grad_total],
    )
    return new_spectrum, grad


def solution(mesh):
    in_specs = (P(None, "slab", None), P(None, "slab", None), P("led", "slab", None), P(), P())
    out_specs = (P(None, "slab", None), P(None, "slab", None))
    return jax.shard_map(per_device, mesh=mesh, in_specs=in_specs, out_specs=out_specs, check_vma=False)
```

```python
import functools
import math

import jax
import jax.numpy as jnp
import numpy as np
from jax import lax
from jax.experimental import pallas as pl
from jax.experimental.pallas import tpu as pltpu
from jax.sharding import PartitionSpec as P

W = 2048
QUARTER = W // 4
BAND = 64
NC = 3072
AMPLITUDE_FLOOR = 0.5
PUPIL_DAMPING = 0.5
MIB = 1024 * 1024

VMEM = pltpu.VMEM
F32 = jnp.float32
BF16 = jnp.bfloat16


def table():
    rows = np.arange(QUARTER, dtype=np.int64)[:, None]
    cols = np.arange(W, dtype=np.int64)[None, :]
    phases = ((rows * cols) % W).astype(np.float32) * np.float32(2.0 * math.pi / W)
    factor = np.float32(1.0 / math.sqrt(W))
    parts = []
    for res in range(4):
        part = phases[:, res::4]
        parts.append(np.concatenate([np.cos(part) * factor, np.sin(part) * factor], 1))
    return np.stack(parts).astype(jnp.bfloat16)


def low_half(shape):
    return lax.broadcasted_iota(jnp.int32, shape, 1) < BAND


def swap(x):
    return pltpu.roll(x, BAND, 1)


def times_i(x):
    s = swap(x)
    return jnp.where(low_half(x.shape), -s, s)


def dft(x_ref, t_ref, g_ref, sign, emit, chunk=32):
    for res in range(4):
        x = x_ref[pl.ds(res, QUARTER, stride=4), :]
        ix = times_i(x)
        if sign < 0:
            ix = -ix
        operand = jnp.concatenate([x.astype(BF16), ix.astype(BF16)], 0)
        g_ref[res] = jnp.dot(t_ref[res], operand, preferred_element_type=F32)

    def combine(step, carry):
        start = pl.multiple_of(step * chunk, chunk)
        rows = pl.ds(start, chunk)
        g0, g1, g2, g3 = g_ref[0, rows, :], g_ref[1, rows, :], g_ref[2, rows, :], g_ref[3, rows, :]
        h0, h1, h2 = g0 + g2, g0 - g2, g1 + g3
        h3 = times_i(g1 - g3)
        if sign < 0:
            h3 = -h3
        emit(start, h0 + h2)
        emit(QUARTER + start, h1 + h3)
        emit(2 * QUARTER + start, h0 - h2)
        emit(3 * QUARTER + start, h1 - h3)
        return carry

    lax.fori_loop(0, QUARTER // chunk, combine, 0)


def store_rows(ref, chunk=32):
    def emit(start, value):
        ref[pl.ds(pl.multiple_of(start, chunk), chunk), :] = value

    return emit


def turn_blocks(x_ref, out_ref):
    def turn(step, carry):
        base = pl.multiple_of(step * 128, 128)
        turned = x_ref[pl.ds(base, 128), :].T
        a, b = turned[:BAND], turned[BAND:]
        low = low_half(a.shape)
        out_ref[pl.ds(base, BAND), :] = jnp.where(low, a, swap(b)).astype(BF16)
        out_ref[pl.ds(pl.multiple_of(base + BAND, BAND), BAND), :] = jnp.where(low, swap(a), b).astype(BF16)
        return carry

    lax.fori_loop(0, W // 128, turn, 0)


GATHER_TILES = W // 128 + 1
GATHER_ROWS = 32


def gather_kernel(col_ref, spec_ref, out_ref, buf_ref, sem):
    col = col_ref[lax.axis_index("led")]
    tile = col // 128
    lo = col - tile * 128
    first = jnp.minimum(tile, NC // 128 - GATHER_TILES)
    skip = tile - first
    shift = lax.rem(128 - lo, 128)
    groups = 128 // GATHER_ROWS

    def fetch(group):
        rows = pl.ds(group * GATHER_ROWS, GATHER_ROWS)
        columns = pl.ds(pl.multiple_of(first * 128, 128), GATHER_TILES * 128)
        return pltpu.make_async_copy(spec_ref.at[:, rows, columns], buf_ref.at[:, rows, :], sem.at[group])

    for group in range(groups):
        fetch(group).start()

    lanes = lax.broadcasted_iota(jnp.int32, (16, 128), 1)
    keep = lanes < 128 - lo
    low = lanes < BAND
    for group in range(groups):
        fetch(group).wait()

        def step(i, carry):
            row = pl.multiple_of(group * GATHER_ROWS + i * 16, 16)

            def load(k, t):
                t = jnp.minimum(skip + t, GATHER_TILES - 1)
                x = buf_ref[k, pl.ds(row, 16), pl.ds(pl.multiple_of(t * 128, 128), 128)]
                return pltpu.roll(x, shift, 1)

            last = (load(0, 0), load(1, 0))
            for t in range(W // 128):
                nxt = (load(0, t + 1), load(1, t + 1))
                a = jnp.where(keep, last[0], nxt[0])
                b = jnp.where(keep, last[1], nxt[1])
                out_ref[pl.ds(pl.multiple_of(row + t * 256, 16), 16), :] = jnp.where(low, a, swap(b)).astype(BF16)
                out_ref[pl.ds(pl.multiple_of(row + t * 256 + 128, 16), 16), :] = jnp.where(
                    low, swap(a), b
                ).astype(BF16)
                last = nxt
            return carry

        lax.fori_loop(0, GATHER_ROWS // 16, step, 0)


def prepare_kernel(pupil_ref, intensity_ref, pr_ref, pi_ref, root_ref):
    def step(t, carry):
        rows = pl.ds(pl.multiple_of(t * 128, 128), 128)
        x = jnp.concatenate([pupil_ref[0, :, rows], pupil_ref[1, :, rows]], 0).T
        s = swap(x)
        low = low_half(x.shape)
        pr_ref[rows, :] = jnp.where(low, x, s)
        pi_ref[rows, :] = jnp.where(low, -s, x)
        v = jnp.sqrt(intensity_ref[0, :, rows])
        root_ref[rows, :] = jnp.concatenate([v, v], 0).T
        return carry

    lax.fori_loop(0, W // 128, step, 0)


def first_kernel(row_ref, recv_ref, pr_ref, pi_ref, t_ref, out_ref, win_ref, wide_ref, x_ref, g_ref):
    row = row_ref[lax.axis_index("led")]
    base = jnp.minimum(row // 16 * 16, 2 * W - (W + 16))
    off = row - base

    def widen(step, carry):
        src = pl.ds(pl.multiple_of(base + step * 48, 16), 48)
        wide_ref[pl.ds(pl.multiple_of(step * 48, 16), 48), :] = recv_ref[src, :].astype(F32)
        return carry

    lax.fori_loop(0, (W + 16) // 48, widen, 0)

    def multiply(step, carry):
        rows = pl.ds(pl.multiple_of(step * 32, 32), 32)
        w = wide_ref[pl.ds(off + step * 32, 32), :]
        product = w * pr_ref[rows, :] + swap(w) * pi_ref[rows, :]
        win_ref[rows, :] = w.astype(BF16)
        x_ref[rows, :] = product.astype(BF16).astype(F32)
        return carry

    lax.fori_loop(0, W // 32, multiply, 0)
    dft(x_ref, t_ref, g_ref, 1, store_rows(x_ref))
    turn_blocks(x_ref, out_ref)


def widen_rows(recv_ref, x_ref):
    def widen(step, carry):
        rows = pl.ds(pl.multiple_of(step * 64, 64), 64)
        x_ref[rows, :] = recv_ref[rows, :].astype(F32)
        return carry

    lax.fori_loop(0, W // 64, widen, 0)


def middle_kernel(recv_ref, root_ref, t_ref, out_ref, x_ref, g_ref):
    widen_rows(recv_ref, x_ref)

    def replace(start, value):
        squared = value * value
        magnitude = jnp.sqrt(squared + swap(squared))
        rows = pl.ds(pl.multiple_of(start, 32), 32)
        scaling = root_ref[rows, :] / jnp.maximum(magnitude, AMPLITUDE_FLOOR)
        x_ref[rows, :] = (value * scaling).astype(BF16).astype(F32)

    dft(x_ref, t_ref, g_ref, 1, replace)
    dft(x_ref, t_ref, g_ref, -1, store_rows(x_ref))
    turn_blocks(x_ref, out_ref)


def last_kernel(row_ref, recv_ref, win_ref, pr_ref, pi_ref, t_ref, grad_ref, corr_ref, x_ref, c_ref, g_ref):
    row = row_ref[lax.axis_index("led")]
    widen_rows(recv_ref, x_ref)

    def update(start, estimate):
        rows = pl.ds(pl.multiple_of(start, 32), 32)
        w = win_ref[rows, :].astype(F32)
        pr, pi = pr_ref[rows, :], pi_ref[rows, :]
        ws = swap(w)
        low = low_half(w.shape)
        change = estimate - (w * pr + ws * pi)
        cs = swap(change)
        wr = jnp.where(low, w, ws)
        wi = jnp.where(low, ws, -w)
        grad_ref[rows, :] = (change * wr + cs * wi).astype(BF16)
        c_ref[pl.ds(row + start, 32), :] = (change * pr - cs * pi) / (pr * pr + pi * pi + PUPIL_DAMPING)

    dft(x_ref, t_ref, g_ref, -1, update)

    def store(step, carry):
        start = pl.multiple_of(step * 64, 64)
        beyond = c_ref[pl.ds(pl.multiple_of(start + W, 64), 64), :]
        within = c_ref[pl.ds(start, 64), :]
        classes = start + lax.broadcasted_iota(jnp.int32, (64, 128), 0)
        dest = (step % 2) * 16 + step // 2
        corr_ref[pl.ds(pl.multiple_of(dest * 64, 64), 64), :] = jnp.where(classes < row, beyond, within).astype(BF16)
        return carry

    lax.fori_loop(0, 32, store, 0)


def reduce_kernel(row_ref, col_ref, recv_ref, own_ref, other_ref, acc_ref):
    slab, led = lax.axis_index("slab"), lax.axis_index("led")
    upper = slab // 16
    base = (slab % 16) * 128 + upper * 64 + led * 8
    acc_ref[...] = jnp.zeros_like(acc_ref)
    lanes = lax.broadcasted_iota(jnp.int32, (16, 128), 1)
    low = lax.broadcasted_iota(jnp.int32, (8, 128), 1) < BAND
    classes = base + lax.rem(lax.broadcasted_iota(jnp.int32, (16, 128), 0), 8)

    def pair(p, carry):
        for j in range(2):
            row, col = row_ref[2 * p + j], col_ref[2 * p + j]
            tile = col // 128
            lo = col - tile * 128
            take = lanes >= lo
            mine = (classes < row) == (upper == 1)

            def put(t, value):
                rows = pl.ds(pl.multiple_of((tile + t) * 16, 16), 16)
                acc_ref[0, rows, :] += jnp.where(mine, value, 0.0)
                acc_ref[1, rows, :] += jnp.where(mine, 0.0, value)

            last = jnp.zeros((16, 128), F32)
            for t in range(W // 128):
                at = pl.multiple_of(t * 128 + p * 16, 16)
                x = recv_ref[pl.ds(at, 16), :].astype(F32)[8 * j : 8 * j + 8]
                y = recv_ref[pl.ds(pl.multiple_of(at + 64, 16), 16), :].astype(F32)[8 * j : 8 * j + 8]
                both = jnp.concatenate([jnp.where(low, x, swap(y)), jnp.where(low, swap(x), y)], 0)
                both = pltpu.roll(both, lo, 1)
                put(t, jnp.where(take, both, last))
                last = both
            put(W // 128, jnp.where(take, 0.0, last))
        return carry

    lax.fori_loop(0, 4, pair, 0)

    def store(t, carry):
        rows = pl.ds(pl.multiple_of(t * 16, 16), 16)
        own_ref[rows, :] = acc_ref[0, rows, :].astype(BF16)
        other_ref[rows, :] = acc_ref[1, rows, :].astype(BF16)
        return carry

    lax.fori_loop(0, NC // 128, store, 0)


HOPS = (0, 1, -1, 2, -2, 3, -3, 4)


def finish_kernel(spec_ref, *refs):
    own, swapped, grads, (new_ref, out_ref) = refs[:8], refs[8:16], refs[16:24], refs[24:]
    slab, led = lax.axis_index("slab"), lax.axis_index("led")
    upper = slab // 16
    for hop, own_ref, swapped_ref, grad_ref in zip(HOPS, own, swapped, grads):
        source = lax.rem(led - hop + 8, 8)
        for half, ref in ((upper, own_ref), (1 - upper, swapped_ref)):
            rows = pl.ds(pl.multiple_of(half * 64 + source * 8, 8), 8)
            for t in range(NC // 128):
                x = ref[t * 16 : t * 16 + 16, :].astype(F32)
                columns = slice(t * 128, t * 128 + 128)
                new_ref[0, rows, columns] = spec_ref[0, rows, columns] + x[:8]
                new_ref[1, rows, columns] = spec_ref[1, rows, columns] + x[8:]
        for t in range(2):
            x = grad_ref[t * 128 : t * 128 + 128, :].astype(F32).T
            columns = pl.ds(pl.multiple_of(source * 256 + t * 128, 128), 128)
            out_ref[0, :, columns] = x[:BAND]
            out_ref[1, :, columns] = x[BAND:]


def call(kernel, outs, scalars, arrays, scratch=(), flops=0, limit=20 * MIB, space=VMEM):
    shapes = [jax.ShapeDtypeStruct(s, d) for s, d in outs]
    moved = sum(math.prod(s) * jnp.dtype(d).itemsize for s, d in outs)
    moved += sum(a.size * a.dtype.itemsize for a in arrays)
    return pl.pallas_call(
        kernel,
        out_shape=shapes,
        in_specs=[pl.BlockSpec(memory_space=pltpu.SMEM)] * len(scalars)
        + [pl.BlockSpec(memory_space=space)] * len(arrays),
        out_specs=[pl.BlockSpec(memory_space=VMEM)] * len(outs),
        scratch_shapes=list(scratch),
        compiler_params=pltpu.CompilerParams(vmem_limit_bytes=limit),
        cost_estimate=pl.CostEstimate(flops=flops, bytes_accessed=moved, transcendentals=0),
    )(*scalars, *arrays)


def turn_bands(values):
    blocks = values.reshape(32, -1, 128)
    return lax.all_to_all(blocks, "slab", 0, 0).reshape(-1, 128)


FORWARD = [(i, (i + 1) % 8) for i in range(8)]
BACKWARD = [(i, (i - 1) % 8) for i in range(8)]


def ring_gather(piece):
    forward = backward = piece
    found = [piece]
    for hop in range(1, 5):
        forward = lax.ppermute(forward, "led", FORWARD)
        found.append(forward)
        if hop < 4:
            backward = lax.ppermute(backward, "led", BACKWARD)
            found.append(backward)
    return found


def per_device(spectrum, pupil, intensity, row_offsets, col_offsets):
    tab = jnp.asarray(table())
    rows128 = (W, 128)
    flops = 8 * QUARTER * 1024 * 128

    (outgoing,) = call(
        gather_kernel,
        [((2 * W, 128), BF16)],
        [col_offsets],
        [spectrum],
        [VMEM((2, 128, GATHER_TILES * 128), F32), pltpu.SemaphoreType.DMA((128 // GATHER_ROWS,))],
        limit=56 * MIB,
        space=pl.ANY,
    )
    arrived = turn_bands(outgoing)
    pr, pi, root = call(prepare_kernel, [(rows128, F32)] * 3, [], [pupil, intensity])
    scratch = [VMEM(rows128, F32), VMEM((4, QUARTER, 128), F32)]
    first, window = call(
        first_kernel,
        [(rows128, BF16), (rows128, BF16)],
        [row_offsets],
        [arrived, pr, pi, tab],
        [VMEM((W + 16, 128), F32)] + scratch,
        flops,
    )
    turned = turn_bands(first)
    (second,) = call(middle_kernel, [(rows128, BF16)], [], [turned, root, tab], scratch, 2 * flops)
    returned = turn_bands(second)
    gradient, correction = call(
        last_kernel,
        [(rows128, BF16), (rows128, BF16)],
        [row_offsets],
        [returned, window, pr, pi, tab],
        [VMEM(rows128, F32), VMEM((2 * W, 128), F32), VMEM((4, QUARTER, 128), F32)],
        flops,
    )
    grad_part = lax.psum_scatter(gradient.reshape(8, W // 8, 128), "led", scatter_dimension=0)
    landed = lax.all_to_all(correction.reshape(256, 8, 128), ("slab", "led"), 0, 0).reshape(rows128)
    piece = (NC // 128 * 16, 128)
    own, other = call(
        reduce_kernel,
        [(piece, BF16), (piece, BF16)],
        [row_offsets, col_offsets],
        [landed],
        [VMEM((2, (NC // 128 + 1) * 16, 128), F32)],
    )
    swapped = lax.ppermute(other, "slab", [(i, (i + 16) % 32) for i in range(32)])
    new_spectrum, grad = call(
        finish_kernel,
        [((2, 128, NC), F32), ((2, BAND, W), F32)],
        [],
        [spectrum, *ring_gather(own), *ring_gather(swapped), *ring_gather(grad_part)],
    )
    return new_spectrum, grad


def solution(mesh):
    in_specs = (P(None, "slab", None), P(None, "slab", None), P("led", "slab", None), P(), P())
    out_specs = (P(None, "slab", None), P(None, "slab", None))
    return jax.shard_map(per_device, mesh=mesh, in_specs=in_specs, out_specs=out_specs, check_vma=False)
```

```python
import functools
import math

import jax
import jax.numpy as jnp
import numpy as np
from jax import lax
from jax.experimental import pallas as pl
from jax.experimental.pallas import tpu as pltpu
from jax.sharding import PartitionSpec as P

W = 2048
QUARTER = W // 4
BAND = 64
NC = 3072
AMPLITUDE_FLOOR = 0.5
PUPIL_DAMPING = 0.5
MIB = 1024 * 1024

VMEM = pltpu.VMEM
F32 = jnp.float32
BF16 = jnp.bfloat16


def table():
    rows = np.arange(QUARTER, dtype=np.int64)[:, None]
    cols = np.arange(W, dtype=np.int64)[None, :]
    phases = ((rows * cols) % W).astype(np.float32) * np.float32(2.0 * math.pi / W)
    factor = np.float32(1.0 / math.sqrt(W))
    parts = []
    for res in range(4):
        part = phases[:, res::4]
        parts.append(np.concatenate([np.cos(part) * factor, np.sin(part) * factor], 1))
    return np.stack(parts).astype(jnp.bfloat16)


def low_half(shape):
    return lax.broadcasted_iota(jnp.int32, shape, 1) < BAND


def swap(x):
    return pltpu.roll(x, BAND, 1)


def times_i(x):
    s = swap(x)
    return jnp.where(low_half(x.shape), -s, s)


def dft(x_ref, t_ref, g_ref, sign, emit, chunk=64):
    for res in range(4):
        x = x_ref[pl.ds(res, QUARTER, stride=4), :]
        ix = times_i(x)
        if sign < 0:
            ix = -ix
        operand = jnp.concatenate([x.astype(BF16), ix.astype(BF16)], 0)
        g_ref[res] = jnp.dot(t_ref[res], operand, preferred_element_type=F32)

    for start in range(0, QUARTER, chunk):
        g0, g1, g2, g3 = (g_ref[res, start : start + chunk, :] for res in range(4))
        h0, h1, h2 = g0 + g2, g0 - g2, g1 + g3
        h3 = times_i(g1 - g3)
        if sign < 0:
            h3 = -h3
        emit(start, h0 + h2)
        emit(QUARTER + start, h1 + h3)
        emit(2 * QUARTER + start, h0 - h2)
        emit(3 * QUARTER + start, h1 - h3)


def store_rows(ref):
    def emit(start, value):
        ref[start : start + value.shape[0], :] = value

    return emit


def turn_blocks(x_ref, out_ref):
    for base in range(0, W, 128):
        turned = x_ref[base : base + 128, :].T
        a, b = turned[:BAND], turned[BAND:]
        low = low_half(a.shape)
        out_ref[base : base + BAND, :] = jnp.where(low, a, swap(b)).astype(BF16)
        out_ref[base + BAND : base + 128, :] = jnp.where(low, swap(a), b).astype(BF16)


def gather_kernel(col_ref, spec_ref, out_ref, x_ref):
    col = col_ref[lax.axis_index("led")]
    tile = col // 128
    lo = col - tile * 128
    for t in range(W // 128 + 1):
        source = jnp.minimum(tile + t, NC // 128 - 1)
        x_ref[:, :, t * 128 : t * 128 + 128] = spec_ref[:, :, pl.ds(pl.multiple_of(source * 128, 128), 128)].astype(BF16)
    source = lax.broadcasted_iota(jnp.int32, (512, 256), 0)
    target = lax.broadcasted_iota(jnp.int32, (512, 256), 1)
    moves = (source % 256 == lo + target // 128 * 64 + target % 64) & (source // 256 == target % 128 // 64)
    moves = moves.astype(F32).astype(BF16)
    for t in range(W // 128):
        columns = slice(t * 128, t * 128 + 256)
        both = jnp.concatenate([x_ref[0, :, columns], x_ref[1, :, columns]], 1)
        moved = jnp.dot(both, moves, preferred_element_type=F32)
        out_ref[t * 256 : t * 256 + 128, :] = moved[:, :128].astype(BF16)
        out_ref[t * 256 + 128 : t * 256 + 256, :] = moved[:, 128:].astype(BF16)


def first_kernel(row_ref, recv_ref, pupil_ref, t_ref, out_ref, win_ref, pr_ref, pi_ref, wide_ref, x_ref, g_ref):
    row = row_ref[lax.axis_index("led")]
    base = jnp.minimum(row // 16 * 16, 2 * W - (W + 16))
    off = row - base
    wide_ref[...] = recv_ref[pl.ds(pl.multiple_of(base, 16), W + 16), :].astype(F32)
    for start in range(0, W, 128):
        rows = slice(start, start + 128)
        x = jnp.concatenate([pupil_ref[0, :, rows], pupil_ref[1, :, rows]], 0).T
        s = swap(x)
        low = low_half(x.shape)
        pr, pi = jnp.where(low, x, s), jnp.where(low, -s, x)
        pr_ref[rows, :] = pr
        pi_ref[rows, :] = pi
        w = wide_ref[pl.ds(off + start, 128), :]
        win_ref[rows, :] = w.astype(BF16)
        x_ref[rows, :] = (w * pr + swap(w) * pi).astype(BF16).astype(F32)
    dft(x_ref, t_ref, g_ref, 1, store_rows(x_ref))
    turn_blocks(x_ref, out_ref)


def middle_kernel(recv_ref, intensity_ref, t_ref, out_ref, root_ref, x_ref, g_ref):
    x_ref[...] = recv_ref[...].astype(F32)
    for start in range(0, W, 128):
        rows = slice(start, start + 128)
        root = jnp.sqrt(intensity_ref[0, :, rows])
        root_ref[rows, :] = jnp.concatenate([root, root], 0).T

    def replace(start, value):
        squared = value * value
        magnitude = jnp.sqrt(squared + swap(squared))
        rows = slice(start, start + value.shape[0])
        scaling = root_ref[rows, :] / jnp.maximum(magnitude, AMPLITUDE_FLOOR)
        x_ref[rows, :] = (value * scaling).astype(BF16).astype(F32)

    dft(x_ref, t_ref, g_ref, 1, replace)
    dft(x_ref, t_ref, g_ref, -1, store_rows(x_ref))
    turn_blocks(x_ref, out_ref)


def last_kernel(row_ref, recv_ref, win_ref, pr_ref, pi_ref, t_ref, grad_ref, corr_ref, x_ref, c_ref, g_ref):
    row = row_ref[lax.axis_index("led")]
    x_ref[...] = recv_ref[...].astype(F32)

    def update(start, estimate):
        size = estimate.shape[0]
        rows = slice(start, start + size)
        w = win_ref[rows, :].astype(F32)
        pr, pi = pr_ref[rows, :], pi_ref[rows, :]
        ws = swap(w)
        low = low_half(w.shape)
        change = estimate - (w * pr + ws * pi)
        cs = swap(change)
        wr = jnp.where(low, w, ws)
        wi = jnp.where(low, ws, -w)
        grad_ref[rows, :] = change * wr + cs * wi
        c_ref[pl.ds(row + start, size), :] = (change * pr - cs * pi) / (pr * pr + pi * pi + PUPIL_DAMPING)

    dft(x_ref, t_ref, g_ref, -1, update)

    for part in range(32):
        start = part * 64
        classes = start + lax.broadcasted_iota(jnp.int32, (64, 128), 0)
        value = jnp.where(classes < row, c_ref[start + W : start + W + 64, :], c_ref[start : start + 64, :])
        dest = (part % 2) * 16 + part // 2
        corr_ref[dest * 64 : dest * 64 + 64, :] = value.astype(BF16)


def reduce_kernel(row_ref, col_ref, recv_ref, own_ref, other_ref, acc_ref):
    slab, led = lax.axis_index("slab"), lax.axis_index("led")
    upper = slab // 16
    base = (slab % 16) * 128 + upper * 64 + led * 8
    acc_ref[...] = jnp.zeros_like(acc_ref)
    lanes = lax.broadcasted_iota(jnp.int32, (16, 128), 1)
    low = lax.broadcasted_iota(jnp.int32, (8, 128), 1) < BAND
    classes = base + lax.rem(lax.broadcasted_iota(jnp.int32, (16, 128), 0), 8)

    def pair(p, carry):
        for j in range(2):
            row, col = row_ref[2 * p + j], col_ref[2 * p + j]
            tile = col // 128
            lo = col - tile * 128
            take = lanes >= lo
            mine = (classes < row) == (upper == 1)

            def put(t, value):
                rows = pl.ds(pl.multiple_of((tile + t) * 16, 16), 16)
                acc_ref[0, rows, :] += jnp.where(mine, value, 0.0)
                acc_ref[1, rows, :] += jnp.where(mine, 0.0, value)

            last = jnp.zeros((16, 128), F32)
            for t in range(W // 128):
                at = pl.multiple_of(t * 128 + p * 16, 16)
                x = recv_ref[pl.ds(at, 16), :].astype(F32)[8 * j : 8 * j + 8]
                y = recv_ref[pl.ds(pl.multiple_of(at + 64, 16), 16), :].astype(F32)[8 * j : 8 * j + 8]
                both = jnp.concatenate([jnp.where(low, x, swap(y)), jnp.where(low, swap(x), y)], 0)
                both = pltpu.roll(both, lo, 1)
                put(t, jnp.where(take, both, last))
                last = both
            put(W // 128, jnp.where(take, 0.0, last))
        return carry

    lax.fori_loop(0, 4, pair, 0)
    own_ref[...] = acc_ref[0, : NC // 8, :].astype(BF16)
    other_ref[...] = acc_ref[1, : NC // 8, :].astype(BF16)


def merge_kernel(swapped_ref, grad_ref, after_ref, out_ref):
    out_ref[: NC // 8, :] = swapped_ref[...]
    out_ref[NC // 8 :, :] = grad_ref[...].astype(BF16)


HOPS = (0, 1, -1, 2, -2, 3, -3, 4)


def finish_kernel(spec_ref, *refs):
    own, rest, (new_ref, out_ref) = refs[:8], refs[8:16], refs[16:]
    slab, led = lax.axis_index("slab"), lax.axis_index("led")
    upper = slab // 16
    for hop, own_ref, rest_ref in zip(HOPS, own, rest):
        source = lax.rem(led - hop + 8, 8)
        for half, ref in ((upper, own_ref), (1 - upper, rest_ref)):
            rows = pl.ds(pl.multiple_of(half * 64 + source * 8, 8), 8)
            for t in range(NC // 128):
                x = ref[t * 16 : t * 16 + 16, :].astype(F32)
                columns = slice(t * 128, t * 128 + 128)
                new_ref[0, rows, columns] = spec_ref[0, rows, columns] + x[:8]
                new_ref[1, rows, columns] = spec_ref[1, rows, columns] + x[8:]
        for t in range(2):
            start = NC // 8 + t * 128
            x = rest_ref[start : start + 128, :].astype(F32).T
            columns = pl.ds(pl.multiple_of(source * 256 + t * 128, 128), 128)
            out_ref[0, :, columns] = x[:BAND]
            out_ref[1, :, columns] = x[BAND:]


def call(kernel, outs, scalars, arrays, scratch=(), flops=0, limit=20 * MIB):
    shapes = [jax.ShapeDtypeStruct(s, d) for s, d in outs]
    moved = sum(math.prod(s) * jnp.dtype(d).itemsize for s, d in outs)
    moved += sum(a.size * a.dtype.itemsize for a in arrays)
    return pl.pallas_call(
        kernel,
        out_shape=shapes,
        in_specs=[pl.BlockSpec(memory_space=pltpu.SMEM)] * len(scalars)
        + [pl.BlockSpec(memory_space=VMEM)] * len(arrays),
        out_specs=[pl.BlockSpec(memory_space=VMEM)] * len(outs),
        scratch_shapes=list(scratch),
        compiler_params=pltpu.CompilerParams(vmem_limit_bytes=limit),
        cost_estimate=pl.CostEstimate(flops=flops, bytes_accessed=moved, transcendentals=0),
    )(*scalars, *arrays)


def turn_bands(values):
    blocks = values.reshape(32, -1, 128)
    return lax.all_to_all(blocks, "slab", 0, 0).reshape(-1, 128)


FORWARD = [(i, (i + 1) % 8) for i in range(8)]
BACKWARD = [(i, (i - 1) % 8) for i in range(8)]


def ring_gather(piece):
    forward = backward = piece
    found = [piece]
    for hop in range(1, 5):
        forward = lax.ppermute(forward, "led", FORWARD)
        found.append(forward)
        if hop < 4:
            backward = lax.ppermute(backward, "led", BACKWARD)
            found.append(backward)
    return found


def per_device(spectrum, pupil, intensity, row_offsets, col_offsets):
    tab = jnp.asarray(table())
    rows128 = (W, 128)
    flops = 8 * QUARTER * 1024 * 128

    (outgoing,) = call(
        gather_kernel, [((2 * W, 128), BF16)], [col_offsets], [spectrum], [VMEM((2, 128, W + 128), BF16)]
    )
    arrived = turn_bands(outgoing)
    scratch = [VMEM(rows128, F32), VMEM((4, QUARTER, 128), F32)]
    first, window, pr, pi = call(
        first_kernel,
        [(rows128, BF16), (rows128, BF16), (rows128, F32), (rows128, F32)],
        [row_offsets],
        [arrived, pupil, tab],
        [VMEM((W + 16, 128), F32)] + scratch,
        flops,
    )
    turned = turn_bands(first)
    (second,) = call(
        middle_kernel, [(rows128, BF16)], [], [turned, intensity, tab], [VMEM(rows128, F32)] + scratch, 2 * flops
    )
    returned = turn_bands(second)
    gradient, correction = call(
        last_kernel,
        [(rows128, F32), (rows128, BF16)],
        [row_offsets],
        [returned, window, pr, pi, tab],
        [VMEM(rows128, F32), VMEM((2 * W, 128), F32), VMEM((4, QUARTER, 128), F32)],
        flops,
    )
    grad_part = lax.psum_scatter(gradient.reshape(8, W // 8, 128), "led", scatter_dimension=0)
    landed = lax.all_to_all(correction.reshape(256, 8, 128), ("slab", "led"), 0, 0).reshape(rows128)
    piece = (NC // 128 * 16, 128)
    own, other = call(
        reduce_kernel,
        [(piece, BF16), (piece, BF16)],
        [row_offsets, col_offsets],
        [landed],
        [VMEM((2, (NC // 128 + 1) * 16, 128), F32)],
    )
    swapped = lax.ppermute(other, "slab", [(i, (i + 16) % 32) for i in range(32)])
    own_pieces = ring_gather(own)
    (rest,) = call(
        merge_kernel, [((piece[0] + W // 8, 128), BF16)], [], [swapped, grad_part.reshape(W // 8, 128), own_pieces[1]]
    )
    new_spectrum, grad = call(
        finish_kernel,
        [((2, 128, NC), F32), ((2, BAND, W), F32)],
        [],
        [spectrum, *own_pieces, *ring_gather(rest)],
    )
    return new_spectrum, grad


def solution(mesh):
    in_specs = (P(None, "slab", None), P(None, "slab", None), P("led", "slab", None), P(), P())
    out_specs = (P(None, "slab", None), P(None, "slab", None))
    return jax.shard_map(per_device, mesh=mesh, in_specs=in_specs, out_specs=out_specs, check_vma=False)
```

```python
import functools
import math

import jax
import jax.numpy as jnp
import numpy as np
from jax import lax
from jax.experimental import pallas as pl
from jax.experimental.pallas import tpu as pltpu
from jax.sharding import PartitionSpec as P

W = 2048
QUARTER = W // 4
BAND = 64
NC = 3072
AMPLITUDE_FLOOR = 0.5
PUPIL_DAMPING = 0.5
MIB = 1024 * 1024

VMEM = pltpu.VMEM
F32 = jnp.float32
BF16 = jnp.bfloat16


def table():
    rows = np.arange(QUARTER, dtype=np.int64)[:, None]
    cols = np.arange(W, dtype=np.int64)[None, :]
    phases = ((rows * cols) % W).astype(np.float32) * np.float32(2.0 * math.pi / W)
    factor = np.float32(1.0 / math.sqrt(W))
    parts = []
    for res in range(4):
        part = phases[:, res::4]
        parts.append(np.concatenate([np.cos(part) * factor, np.sin(part) * factor], 1))
    return np.stack(parts).astype(jnp.bfloat16)


def low_half(shape):
    return lax.broadcasted_iota(jnp.int32, shape, 1) < BAND


def swap(x):
    return pltpu.roll(x, BAND, 1)


def times_i(x):
    s = swap(x)
    return jnp.where(low_half(x.shape), -s, s)


def dft(x_ref, t_ref, g_ref, sign, emit, chunk=64):
    for res in range(4):
        x = x_ref[pl.ds(res, QUARTER, stride=4), :]
        ix = times_i(x)
        if sign < 0:
            ix = -ix
        operand = jnp.concatenate([x.astype(BF16), ix.astype(BF16)], 0)
        g_ref[res] = jnp.dot(t_ref[res], operand, preferred_element_type=F32)

    for start in range(0, QUARTER, chunk):
        g0, g1, g2, g3 = (g_ref[res, start : start + chunk, :] for res in range(4))
        h0, h1, h2 = g0 + g2, g0 - g2, g1 + g3
        h3 = times_i(g1 - g3)
        if sign < 0:
            h3 = -h3
        emit(start, h0 + h2)
        emit(QUARTER + start, h1 + h3)
        emit(2 * QUARTER + start, h0 - h2)
        emit(3 * QUARTER + start, h1 - h3)


def store_rows(ref):
    def emit(start, value):
        ref[start : start + value.shape[0], :] = value

    return emit


def turn_blocks(x_ref, out_ref):
    for base in range(0, W, 128):
        turned = x_ref[base : base + 128, :].T
        a, b = turned[:BAND], turned[BAND:]
        low = low_half(a.shape)
        out_ref[base : base + BAND, :] = jnp.where(low, a, swap(b)).astype(BF16)
        out_ref[base + BAND : base + 128, :] = jnp.where(low, swap(a), b).astype(BF16)


def gather_kernel(col_ref, spec_ref, out_ref, x_ref):
    col = col_ref[lax.axis_index("led")]
    tile = col // 128
    lo = col - tile * 128
    for t in range(W // 128 + 1):
        source = jnp.minimum(tile + t, NC // 128 - 1)
        x_ref[:, :, t * 128 : t * 128 + 128] = spec_ref[:, :, pl.ds(pl.multiple_of(source * 128, 128), 128)].astype(BF16)
    source = lax.broadcasted_iota(jnp.int32, (512, 256), 0)
    target = lax.broadcasted_iota(jnp.int32, (512, 256), 1)
    moves = (source % 256 == lo + target // 128 * 64 + target % 64) & (source // 256 == target % 128 // 64)
    moves = moves.astype(F32).astype(BF16)
    for t in range(W // 128):
        columns = slice(t * 128, t * 128 + 256)
        both = jnp.concatenate([x_ref[0, :, columns], x_ref[1, :, columns]], 1)
        moved = jnp.dot(both, moves, preferred_element_type=F32)
        out_ref[t * 256 : t * 256 + 128, :] = moved[:, :128].astype(BF16)
        out_ref[t * 256 + 128 : t * 256 + 256, :] = moved[:, 128:].astype(BF16)


def first_kernel(row_ref, recv_ref, pupil_ref, t_ref, out_ref, win_ref, pr_ref, pi_ref, wide_ref, x_ref, g_ref):
    row = row_ref[lax.axis_index("led")]
    base = jnp.minimum(row // 16 * 16, 2 * W - (W + 16))
    off = row - base
    wide_ref[...] = recv_ref[pl.ds(pl.multiple_of(base, 16), W + 16), :].astype(F32)
    for start in range(0, W, 128):
        rows = slice(start, start + 128)
        x = jnp.concatenate([pupil_ref[0, :, rows], pupil_ref[1, :, rows]], 0).T
        s = swap(x)
        low = low_half(x.shape)
        pr, pi = jnp.where(low, x, s), jnp.where(low, -s, x)
        pr_ref[rows, :] = pr
        pi_ref[rows, :] = pi
        w = wide_ref[pl.ds(off + start, 128), :]
        win_ref[rows, :] = w.astype(BF16)
        x_ref[rows, :] = (w * pr + swap(w) * pi).astype(BF16).astype(F32)
    dft(x_ref, t_ref, g_ref, 1, store_rows(x_ref))
    turn_blocks(x_ref, out_ref)


def middle_kernel(recv_ref, intensity_ref, t_ref, out_ref, root_ref, x_ref, g_ref):
    x_ref[...] = recv_ref[...].astype(F32)
    for start in range(0, W, 128):
        rows = slice(start, start + 128)
        root = jnp.sqrt(intensity_ref[0, :, rows])
        root_ref[rows, :] = jnp.concatenate([root, root], 0).T

    def replace(start, value):
        squared = value * value
        magnitude = jnp.sqrt(squared + swap(squared))
        rows = slice(start, start + value.shape[0])
        scaling = root_ref[rows, :] / jnp.maximum(magnitude, AMPLITUDE_FLOOR)
        x_ref[rows, :] = (value * scaling).astype(BF16).astype(F32)

    dft(x_ref, t_ref, g_ref, 1, replace)
    dft(x_ref, t_ref, g_ref, -1, store_rows(x_ref))
    turn_blocks(x_ref, out_ref)


def last_kernel(row_ref, recv_ref, win_ref, pr_ref, pi_ref, t_ref, grad_ref, corr_ref, x_ref, c_ref, g_ref):
    row = row_ref[lax.axis_index("led")]
    x_ref[...] = recv_ref[...].astype(F32)

    def update(start, estimate):
        size = estimate.shape[0]
        rows = slice(start, start + size)
        w = win_ref[rows, :].astype(F32)
        pr, pi = pr_ref[rows, :], pi_ref[rows, :]
        ws = swap(w)
        low = low_half(w.shape)
        change = estimate - (w * pr + ws * pi)
        cs = swap(change)
        wr = jnp.where(low, w, ws)
        wi = jnp.where(low, ws, -w)
        grad_ref[rows, :] = (change * wr + cs * wi).astype(BF16)
        c_ref[pl.ds(row + start, size), :] = (change * pr - cs * pi) / (pr * pr + pi * pi + PUPIL_DAMPING)

    dft(x_ref, t_ref, g_ref, -1, update)

    for part in range(32):
        start = part * 64
        classes = start + lax.broadcasted_iota(jnp.int32, (64, 128), 0)
        value = jnp.where(classes < row, c_ref[start + W : start + W + 64, :], c_ref[start : start + 64, :])
        dest = (part % 2) * 16 + part // 2
        corr_ref[dest * 64 : dest * 64 + 64, :] = value.astype(BF16)


def reduce_kernel(row_ref, col_ref, recv_ref, grad_ref, own_ref, other_ref, acc_ref):
    slab, led = lax.axis_index("slab"), lax.axis_index("led")
    upper = slab // 16
    base = (slab % 16) * 128 + upper * 64 + led * 8
    acc_ref[...] = jnp.zeros_like(acc_ref)
    lanes = lax.broadcasted_iota(jnp.int32, (16, 128), 1)
    low = lax.broadcasted_iota(jnp.int32, (8, 128), 1) < BAND
    classes = base + lax.rem(lax.broadcasted_iota(jnp.int32, (16, 128), 0), 8)

    def pair(p, carry):
        for j in range(2):
            row, col = row_ref[2 * p + j], col_ref[2 * p + j]
            tile = col // 128
            lo = col - tile * 128
            take = lanes >= lo
            mine = (classes < row) == (upper == 1)

            def put(t, value):
                rows = pl.ds(pl.multiple_of((tile + t) * 16, 16), 16)
                acc_ref[0, rows, :] += jnp.where(mine, value, 0.0)
                acc_ref[1, rows, :] += jnp.where(mine, 0.0, value)

            last = jnp.zeros((16, 128), F32)
            for t in range(W // 128):
                at = pl.multiple_of(t * 128 + p * 16, 16)
                x = recv_ref[pl.ds(at, 16), :].astype(F32)[8 * j : 8 * j + 8]
                y = recv_ref[pl.ds(pl.multiple_of(at + 64, 16), 16), :].astype(F32)[8 * j : 8 * j + 8]
                both = jnp.concatenate([jnp.where(low, x, swap(y)), jnp.where(low, swap(x), y)], 0)
                both = pltpu.roll(both, lo, 1)
                put(t, jnp.where(take, both, last))
                last = both
            put(W // 128, jnp.where(take, 0.0, last))
        return carry

    lax.fori_loop(0, 4, pair, 0)
    own_ref[: NC // 8, :] = acc_ref[0, : NC // 8, :].astype(BF16)
    for start in range(0, W // 8, 64):
        total = grad_ref[start : start + 64, :].astype(F32)
        for j in range(1, 8):
            total += grad_ref[j * (W // 8) + start : j * (W // 8) + start + 64, :].astype(F32)
        own_ref[NC // 8 + start : NC // 8 + start + 64, :] = total.astype(BF16)
    other_ref[...] = acc_ref[1, : NC // 8, :].astype(BF16)


HOPS = (0, 1, -1, 2, -2, 3, -3, 4)


def finish_kernel(spec_ref, *refs):
    own, swapped, (new_ref, out_ref) = refs[:8], refs[8:16], refs[16:]
    slab, led = lax.axis_index("slab"), lax.axis_index("led")
    upper = slab // 16
    for hop, own_ref, swapped_ref in zip(HOPS, own, swapped):
        source = lax.rem(led - hop + 8, 8)
        for half, ref in ((upper, own_ref), (1 - upper, swapped_ref)):
            rows = pl.ds(pl.multiple_of(half * 64 + source * 8, 8), 8)
            for t in range(NC // 128):
                x = ref[t * 16 : t * 16 + 16, :].astype(F32)
                columns = slice(t * 128, t * 128 + 128)
                new_ref[0, rows, columns] = spec_ref[0, rows, columns] + x[:8]
                new_ref[1, rows, columns] = spec_ref[1, rows, columns] + x[8:]
        for t in range(2):
            start = NC // 8 + t * 128
            x = own_ref[start : start + 128, :].astype(F32).T
            columns = pl.ds(pl.multiple_of(source * 256 + t * 128, 128), 128)
            out_ref[0, :, columns] = x[:BAND]
            out_ref[1, :, columns] = x[BAND:]


def call(kernel, outs, scalars, arrays, scratch=(), flops=0, limit=20 * MIB):
    shapes = [jax.ShapeDtypeStruct(s, d) for s, d in outs]
    moved = sum(math.prod(s) * jnp.dtype(d).itemsize for s, d in outs)
    moved += sum(a.size * a.dtype.itemsize for a in arrays)
    return pl.pallas_call(
        kernel,
        out_shape=shapes,
        in_specs=[pl.BlockSpec(memory_space=pltpu.SMEM)] * len(scalars)
        + [pl.BlockSpec(memory_space=VMEM)] * len(arrays),
        out_specs=[pl.BlockSpec(memory_space=VMEM)] * len(outs),
        scratch_shapes=list(scratch),
        compiler_params=pltpu.CompilerParams(vmem_limit_bytes=limit),
        cost_estimate=pl.CostEstimate(flops=flops, bytes_accessed=moved, transcendentals=0),
    )(*scalars, *arrays)


def turn_bands(values):
    blocks = values.reshape(32, -1, 128)
    return lax.all_to_all(blocks, "slab", 0, 0).reshape(-1, 128)


FORWARD = [(i, (i + 1) % 8) for i in range(8)]
BACKWARD = [(i, (i - 1) % 8) for i in range(8)]


def ring_gather(piece):
    forward = backward = piece
    found = [piece]
    for hop in range(1, 5):
        forward = lax.ppermute(forward, "led", FORWARD)
        found.append(forward)
        if hop < 4:
            backward = lax.ppermute(backward, "led", BACKWARD)
            found.append(backward)
    return found


def per_device(spectrum, pupil, intensity, row_offsets, col_offsets):
    tab = jnp.asarray(table())
    rows128 = (W, 128)
    flops = 8 * QUARTER * 1024 * 128

    (outgoing,) = call(
        gather_kernel, [((2 * W, 128), BF16)], [col_offsets], [spectrum], [VMEM((2, 128, W + 128), BF16)]
    )
    arrived = turn_bands(outgoing)
    scratch = [VMEM(rows128, F32), VMEM((4, QUARTER, 128), F32)]
    first, window, pr, pi = call(
        first_kernel,
        [(rows128, BF16), (rows128, BF16), (rows128, F32), (rows128, F32)],
        [row_offsets],
        [arrived, pupil, tab],
        [VMEM((W + 16, 128), F32)] + scratch,
        flops,
    )
    turned = turn_bands(first)
    (second,) = call(
        middle_kernel, [(rows128, BF16)], [], [turned, intensity, tab], [VMEM(rows128, F32)] + scratch, 2 * flops
    )
    returned = turn_bands(second)
    gradient, correction = call(
        last_kernel,
        [(rows128, BF16), (rows128, BF16)],
        [row_offsets],
        [returned, window, pr, pi, tab],
        [VMEM(rows128, F32), VMEM((2 * W, 128), F32), VMEM((4, QUARTER, 128), F32)],
        flops,
    )
    grads = lax.all_to_all(gradient.reshape(8, W // 8, 128), "led", 0, 0).reshape(rows128)
    landed = lax.all_to_all(correction.reshape(256, 8, 128), ("slab", "led"), 0, 0).reshape(rows128)
    piece = NC // 8
    own, other = call(
        reduce_kernel,
        [((piece + W // 8, 128), BF16), ((piece, 128), BF16)],
        [row_offsets, col_offsets],
        [landed, grads],
        [VMEM((2, piece + 16, 128), F32)],
    )
    own_pieces = ring_gather(own)
    swapped = lax.ppermute(other, "slab", [(i, (i + 16) % 32) for i in range(32)])
    return call(
        finish_kernel,
        [((2, 128, NC), F32), ((2, BAND, W), F32)],
        [],
        [spectrum, *own_pieces, *ring_gather(swapped)],
    )


def solution(mesh):
    in_specs = (P(None, "slab", None), P(None, "slab", None), P("led", "slab", None), P(), P())
    out_specs = (P(None, "slab", None), P(None, "slab", None))
    return jax.shard_map(per_device, mesh=mesh, in_specs=in_specs, out_specs=out_specs, check_vma=False)
```

```python
import functools
import math

import jax
import jax.numpy as jnp
import numpy as np
from jax import lax
from jax.experimental import pallas as pl
from jax.experimental.pallas import tpu as pltpu
from jax.sharding import PartitionSpec as P

W = 2048
QUARTER = W // 4
BAND = 64
NC = 3072
AMPLITUDE_FLOOR = 0.5
PUPIL_DAMPING = 0.5
MIB = 1024 * 1024

VMEM = pltpu.VMEM
F32 = jnp.float32
BF16 = jnp.bfloat16


def table():
    rows = np.arange(QUARTER, dtype=np.int64)[:, None]
    cols = np.arange(W, dtype=np.int64)[None, :]
    phases = ((rows * cols) % W).astype(np.float32) * np.float32(2.0 * math.pi / W)
    factor = np.float32(1.0 / math.sqrt(W))
    parts = []
    for res in range(4):
        part = phases[:, res::4]
        parts.append(np.concatenate([np.cos(part) * factor, np.sin(part) * factor], 1))
    return np.stack(parts).astype(jnp.bfloat16)


def low_half(shape):
    return lax.broadcasted_iota(jnp.int32, shape, 1) < BAND


def swap(x):
    return pltpu.roll(x, BAND, 1)


def times_i(x):
    s = swap(x)
    return jnp.where(low_half(x.shape), -s, s)


def dft(x_ref, t_ref, g_ref, sign, emit, chunk=64):
    for res in range(4):
        x = x_ref[pl.ds(res, QUARTER, stride=4), :]
        ix = times_i(x)
        if sign < 0:
            ix = -ix
        operand = jnp.concatenate([x.astype(BF16), ix.astype(BF16)], 0)
        g_ref[res] = jnp.dot(t_ref[res], operand, preferred_element_type=F32)

    for start in range(0, QUARTER, chunk):
        g0, g1, g2, g3 = (g_ref[res, start : start + chunk, :] for res in range(4))
        h0, h1, h2 = g0 + g2, g0 - g2, g1 + g3
        h3 = times_i(g1 - g3)
        if sign < 0:
            h3 = -h3
        emit(start, h0 + h2)
        emit(QUARTER + start, h1 + h3)
        emit(2 * QUARTER + start, h0 - h2)
        emit(3 * QUARTER + start, h1 - h3)


def store_rows(ref):
    def emit(start, value):
        ref[start : start + value.shape[0], :] = value

    return emit


def turn_blocks(x_ref, out_ref):
    for base in range(0, W, 128):
        turned = x_ref[base : base + 128, :].T
        a, b = turned[:BAND], turned[BAND:]
        low = low_half(a.shape)
        out_ref[base : base + BAND, :] = jnp.where(low, a, swap(b)).astype(BF16)
        out_ref[base + BAND : base + 128, :] = jnp.where(low, swap(a), b).astype(BF16)


def gather_kernel(col_ref, spec_ref, out_ref, x_ref):
    col = col_ref[lax.axis_index("led")]
    tile = col // 128
    lo = col - tile * 128
    for t in range(W // 128 + 1):
        source = jnp.minimum(tile + t, NC // 128 - 1)
        x_ref[:, :, t * 128 : t * 128 + 128] = spec_ref[:, :, pl.ds(pl.multiple_of(source * 128, 128), 128)].astype(BF16)
    source = lax.broadcasted_iota(jnp.int32, (512, 256), 0)
    target = lax.broadcasted_iota(jnp.int32, (512, 256), 1)
    moves = (source % 256 == lo + target // 128 * 64 + target % 64) & (source // 256 == target % 128 // 64)
    moves = moves.astype(F32).astype(BF16)
    for t in range(W // 128):
        columns = slice(t * 128, t * 128 + 256)
        both = jnp.concatenate([x_ref[0, :, columns], x_ref[1, :, columns]], 1)
        moved = jnp.dot(both, moves, preferred_element_type=F32)
        out_ref[t * 256 : t * 256 + 128, :] = moved[:, :128].astype(BF16)
        out_ref[t * 256 + 128 : t * 256 + 256, :] = moved[:, 128:].astype(BF16)


def first_kernel(row_ref, recv_ref, pupil_ref, t_ref, out_ref, win_ref, pr_ref, pi_ref, wide_ref, x_ref, g_ref):
    row = row_ref[lax.axis_index("led")]
    base = jnp.minimum(row // 16 * 16, 2 * W - (W + 16))
    off = row - base
    wide_ref[...] = recv_ref[pl.ds(pl.multiple_of(base, 16), W + 16), :].astype(F32)
    for start in range(0, W, 128):
        rows = slice(start, start + 128)
        x = jnp.concatenate([pupil_ref[0, :, rows], pupil_ref[1, :, rows]], 0).T
        s = swap(x)
        low = low_half(x.shape)
        pr, pi = jnp.where(low, x, s), jnp.where(low, -s, x)
        pr_ref[rows, :] = pr
        pi_ref[rows, :] = pi
        w = wide_ref[pl.ds(off + start, 128), :]
        win_ref[rows, :] = w.astype(BF16)
        x_ref[rows, :] = (w * pr + swap(w) * pi).astype(BF16).astype(F32)
    dft(x_ref, t_ref, g_ref, 1, store_rows(x_ref))
    turn_blocks(x_ref, out_ref)


def middle_kernel(recv_ref, intensity_ref, t_ref, out_ref, root_ref, x_ref, g_ref):
    x_ref[...] = recv_ref[...].astype(F32)
    for start in range(0, W, 128):
        rows = slice(start, start + 128)
        root = jnp.sqrt(intensity_ref[0, :, rows])
        root_ref[rows, :] = jnp.concatenate([root, root], 0).T

    def replace(start, value):
        squared = value * value
        magnitude = jnp.sqrt(squared + swap(squared))
        rows = slice(start, start + value.shape[0])
        scaling = root_ref[rows, :] / jnp.maximum(magnitude, AMPLITUDE_FLOOR)
        x_ref[rows, :] = (value * scaling).astype(BF16).astype(F32)

    dft(x_ref, t_ref, g_ref, 1, replace)
    dft(x_ref, t_ref, g_ref, -1, store_rows(x_ref))
    turn_blocks(x_ref, out_ref)


def last_kernel(row_ref, recv_ref, win_ref, pr_ref, pi_ref, t_ref, grad_ref, corr_ref, x_ref, c_ref, g_ref):
    row = row_ref[lax.axis_index("led")]
    x_ref[...] = recv_ref[...].astype(F32)

    def update(start, estimate):
        size = estimate.shape[0]
        rows = slice(start, start + size)
        w = win_ref[rows, :].astype(F32)
        pr, pi = pr_ref[rows, :], pi_ref[rows, :]
        ws = swap(w)
        low = low_half(w.shape)
        change = estimate - (w * pr + ws * pi)
        cs = swap(change)
        wr = jnp.where(low, w, ws)
        wi = jnp.where(low, ws, -w)
        grad_ref[rows, :] = (change * wr + cs * wi).astype(BF16)
        c_ref[pl.ds(row + start, size), :] = (change * pr - cs * pi) / (pr * pr + pi * pi + PUPIL_DAMPING)

    dft(x_ref, t_ref, g_ref, -1, update)

    for part in range(32):
        start = part * 64
        classes = start + lax.broadcasted_iota(jnp.int32, (64, 128), 0)
        value = jnp.where(classes < row, c_ref[start + W : start + W + 64, :], c_ref[start : start + 64, :])
        dest = (part % 2) * 16 + part // 2
        corr_ref[dest * 64 : dest * 64 + 64, :] = value.astype(BF16)


def reduce_kernel(row_ref, col_ref, recv_ref, own_ref, other_ref, acc_ref):
    slab, led = lax.axis_index("slab"), lax.axis_index("led")
    upper = slab // 16
    base = (slab % 16) * 128 + upper * 64 + led * 8
    acc_ref[...] = jnp.zeros_like(acc_ref)
    lanes = lax.broadcasted_iota(jnp.int32, (16, 128), 1)
    low = lax.broadcasted_iota(jnp.int32, (8, 128), 1) < BAND
    classes = base + lax.rem(lax.broadcasted_iota(jnp.int32, (16, 128), 0), 8)

    def pair(p, carry):
        for j in range(2):
            row, col = row_ref[2 * p + j], col_ref[2 * p + j]
            tile = col // 128
            lo = col - tile * 128
            take = lanes >= lo
            mine = (classes < row) == (upper == 1)

            def put(t, value):
                rows = pl.ds(pl.multiple_of((tile + t) * 16, 16), 16)
                acc_ref[0, rows, :] += jnp.where(mine, value, 0.0)
                acc_ref[1, rows, :] += jnp.where(mine, 0.0, value)

            last = jnp.zeros((16, 128), F32)
            for t in range(W // 128):
                at = pl.multiple_of(t * 128 + p * 16, 16)
                x = recv_ref[pl.ds(at, 16), :].astype(F32)[8 * j : 8 * j + 8]
                y = recv_ref[pl.ds(pl.multiple_of(at + 64, 16), 16), :].astype(F32)[8 * j : 8 * j + 8]
                both = jnp.concatenate([jnp.where(low, x, swap(y)), jnp.where(low, swap(x), y)], 0)
                both = pltpu.roll(both, lo, 1)
                put(t, jnp.where(take, both, last))
                last = both
            put(W // 128, jnp.where(take, 0.0, last))
        return carry

    lax.fori_loop(0, 4, pair, 0)
    own_ref[...] = acc_ref[0, : NC // 8, :].astype(BF16)
    other_ref[...] = acc_ref[1, : NC // 8, :].astype(BF16)


def merge_kernel(grad_ref, swapped_ref, *refs):
    out_ref = refs[-1]
    out_ref[: NC // 8, :] = swapped_ref[...]
    for start in range(0, W // 8, 64):
        total = grad_ref[start : start + 64, :].astype(F32)
        for j in range(1, 8):
            total += grad_ref[j * (W // 8) + start : j * (W // 8) + start + 64, :].astype(F32)
        out_ref[NC // 8 + start : NC // 8 + start + 64, :] = total.astype(BF16)


HOPS = (0, 1, -1, 2, -2, 3, -3, 4)


def finish_kernel(spec_ref, *refs):
    own, swapped, (new_ref, out_ref) = refs[:8], refs[8:16], refs[16:]
    slab, led = lax.axis_index("slab"), lax.axis_index("led")
    upper = slab // 16
    for hop, own_ref, swapped_ref in zip(HOPS, own, swapped):
        source = lax.rem(led - hop + 8, 8)
        for half, ref in ((upper, own_ref), (1 - upper, swapped_ref)):
            rows = pl.ds(pl.multiple_of(half * 64 + source * 8, 8), 8)
            for t in range(NC // 128):
                x = ref[t * 16 : t * 16 + 16, :].astype(F32)
                columns = slice(t * 128, t * 128 + 128)
                new_ref[0, rows, columns] = spec_ref[0, rows, columns] + x[:8]
                new_ref[1, rows, columns] = spec_ref[1, rows, columns] + x[8:]
        for t in range(2):
            start = NC // 8 + t * 128
            x = swapped_ref[start : start + 128, :].astype(F32).T
            columns = pl.ds(pl.multiple_of(source * 256 + t * 128, 128), 128)
            out_ref[0, :, columns] = x[:BAND]
            out_ref[1, :, columns] = x[BAND:]


def call(kernel, outs, scalars, arrays, scratch=(), flops=0, limit=20 * MIB):
    shapes = [jax.ShapeDtypeStruct(s, d) for s, d in outs]
    moved = sum(math.prod(s) * jnp.dtype(d).itemsize for s, d in outs)
    moved += sum(a.size * a.dtype.itemsize for a in arrays)
    return pl.pallas_call(
        kernel,
        out_shape=shapes,
        in_specs=[pl.BlockSpec(memory_space=pltpu.SMEM)] * len(scalars)
        + [pl.BlockSpec(memory_space=VMEM)] * len(arrays),
        out_specs=[pl.BlockSpec(memory_space=VMEM)] * len(outs),
        scratch_shapes=list(scratch),
        compiler_params=pltpu.CompilerParams(vmem_limit_bytes=limit),
        cost_estimate=pl.CostEstimate(flops=flops, bytes_accessed=moved, transcendentals=0),
    )(*scalars, *arrays)


def turn_bands(values):
    blocks = values.reshape(32, -1, 128)
    return lax.all_to_all(blocks, "slab", 0, 0).reshape(-1, 128)


FORWARD = [(i, (i + 1) % 8) for i in range(8)]
BACKWARD = [(i, (i - 1) % 8) for i in range(8)]


def ring_gather(piece):
    forward = backward = piece
    found = [piece]
    for hop in range(1, 5):
        forward = lax.ppermute(forward, "led", FORWARD)
        found.append(forward)
        if hop < 4:
            backward = lax.ppermute(backward, "led", BACKWARD)
            found.append(backward)
    return found


def per_device(spectrum, pupil, intensity, row_offsets, col_offsets):
    tab = jnp.asarray(table())
    rows128 = (W, 128)
    flops = 8 * QUARTER * 1024 * 128

    (outgoing,) = call(
        gather_kernel, [((2 * W, 128), BF16)], [col_offsets], [spectrum], [VMEM((2, 128, W + 128), BF16)]
    )
    arrived = turn_bands(outgoing)
    scratch = [VMEM(rows128, F32), VMEM((4, QUARTER, 128), F32)]
    first, window, pr, pi = call(
        first_kernel,
        [(rows128, BF16), (rows128, BF16), (rows128, F32), (rows128, F32)],
        [row_offsets],
        [arrived, pupil, tab],
        [VMEM((W + 16, 128), F32)] + scratch,
        flops,
    )
    turned = turn_bands(first)
    (second,) = call(
        middle_kernel, [(rows128, BF16)], [], [turned, intensity, tab], [VMEM(rows128, F32)] + scratch, 2 * flops
    )
    returned = turn_bands(second)
    gradient, correction = call(
        last_kernel,
        [(rows128, BF16), (rows128, BF16)],
        [row_offsets],
        [returned, window, pr, pi, tab],
        [VMEM(rows128, F32), VMEM((2 * W, 128), F32), VMEM((4, QUARTER, 128), F32)],
        flops,
    )
    landed = lax.all_to_all(correction.reshape(256, 8, 128), ("slab", "led"), 0, 0).reshape(rows128)
    gradient, landed = lax.optimization_barrier((gradient, landed))
    piece = NC // 8
    own, other = call(
        reduce_kernel,
        [((piece, 128), BF16)] * 2,
        [row_offsets, col_offsets],
        [landed],
        [VMEM((2, piece + 16, 128), F32)],
    )
    swapped = lax.ppermute(other, "slab", [(i, (i + 16) % 32) for i in range(32)])
    grads = lax.all_to_all(gradient.reshape(8, W // 8, 128), "led", 0, 0).reshape(rows128)
    own_pieces = ring_gather(own)
    (rest,) = call(merge_kernel, [((piece + W // 8, 128), BF16)], [], [grads, swapped, *own_pieces[1:3]])
    return call(
        finish_kernel,
        [((2, 128, NC), F32), ((2, BAND, W), F32)],
        [],
        [spectrum, *own_pieces, *ring_gather(rest)],
    )


def solution(mesh):
    in_specs = (P(None, "slab", None), P(None, "slab", None), P("led", "slab", None), P(), P())
    out_specs = (P(None, "slab", None), P(None, "slab", None))
    return jax.shard_map(per_device, mesh=mesh, in_specs=in_specs, out_specs=out_specs, check_vma=False)
```

```python
import functools
import math

import jax
import jax.numpy as jnp
import numpy as np
from jax import lax
from jax.experimental import pallas as pl
from jax.experimental.pallas import tpu as pltpu
from jax.sharding import PartitionSpec as P

W = 2048
QUARTER = W // 4
BAND = 64
NC = 3072
AMPLITUDE_FLOOR = 0.5
PUPIL_DAMPING = 0.5
MIB = 1024 * 1024

VMEM = pltpu.VMEM
F32 = jnp.float32
BF16 = jnp.bfloat16


def table():
    rows = np.arange(QUARTER, dtype=np.int64)[:, None]
    cols = np.arange(W, dtype=np.int64)[None, :]
    phases = ((rows * cols) % W).astype(np.float32) * np.float32(2.0 * math.pi / W)
    factor = np.float32(1.0 / math.sqrt(W))
    parts = []
    for res in range(4):
        part = phases[:, res::4]
        parts.append(np.concatenate([np.cos(part) * factor, np.sin(part) * factor], 1))
    return np.stack(parts).astype(jnp.bfloat16)


def low_half(shape):
    return lax.broadcasted_iota(jnp.int32, shape, 1) < BAND


def swap(x):
    return pltpu.roll(x, BAND, 1)


def times_i(x):
    s = swap(x)
    return jnp.where(low_half(x.shape), -s, s)


def dft(x_ref, t_ref, g_ref, sign, emit, chunk=64):
    for res in range(4):
        x = x_ref[pl.ds(res, QUARTER, stride=4), :]
        ix = times_i(x)
        if sign < 0:
            ix = -ix
        operand = jnp.concatenate([x.astype(BF16), ix.astype(BF16)], 0)
        g_ref[res] = jnp.dot(t_ref[res], operand, preferred_element_type=F32)

    for start in range(0, QUARTER, chunk):
        g0, g1, g2, g3 = (g_ref[res, start : start + chunk, :] for res in range(4))
        h0, h1, h2 = g0 + g2, g0 - g2, g1 + g3
        h3 = times_i(g1 - g3)
        if sign < 0:
            h3 = -h3
        emit(start, h0 + h2)
        emit(QUARTER + start, h1 + h3)
        emit(2 * QUARTER + start, h0 - h2)
        emit(3 * QUARTER + start, h1 - h3)


def store_rows(ref):
    def emit(start, value):
        ref[start : start + value.shape[0], :] = value

    return emit


def turn_blocks(x_ref, out_ref):
    for base in range(0, W, 128):
        turned = x_ref[base : base + 128, :].T
        a, b = turned[:BAND], turned[BAND:]
        low = low_half(a.shape)
        out_ref[base : base + BAND, :] = jnp.where(low, a, swap(b)).astype(BF16)
        out_ref[base + BAND : base + 128, :] = jnp.where(low, swap(a), b).astype(BF16)


def gather_kernel(col_ref, spec_ref, out_ref, x_ref):
    col = col_ref[lax.axis_index("led")]
    tile = col // 128
    lo = col - tile * 128
    for t in range(W // 128 + 1):
        source = jnp.minimum(tile + t, NC // 128 - 1)
        x_ref[:, :, t * 128 : t * 128 + 128] = spec_ref[:, :, pl.ds(pl.multiple_of(source * 128, 128), 128)].astype(BF16)
    source = lax.broadcasted_iota(jnp.int32, (512, 256), 0)
    target = lax.broadcasted_iota(jnp.int32, (512, 256), 1)
    moves = (source % 256 == lo + target // 128 * 64 + target % 64) & (source // 256 == target % 128 // 64)
    moves = moves.astype(F32).astype(BF16)
    for t in range(W // 128):
        columns = slice(t * 128, t * 128 + 256)
        both = jnp.concatenate([x_ref[0, :, columns], x_ref[1, :, columns]], 1)
        moved = jnp.dot(both, moves, preferred_element_type=F32)
        out_ref[t * 256 : t * 256 + 128, :] = moved[:, :128].astype(BF16)
        out_ref[t * 256 + 128 : t * 256 + 256, :] = moved[:, 128:].astype(BF16)


def first_kernel(row_ref, recv_ref, pupil_ref, t_ref, out_ref, win_ref, pr_ref, pi_ref, wide_ref, x_ref, g_ref):
    row = row_ref[lax.axis_index("led")]
    base = jnp.minimum(row // 16 * 16, 2 * W - (W + 16))
    off = row - base
    wide_ref[...] = recv_ref[pl.ds(pl.multiple_of(base, 16), W + 16), :].astype(F32)
    for start in range(0, W, 128):
        rows = slice(start, start + 128)
        x = jnp.concatenate([pupil_ref[0, :, rows], pupil_ref[1, :, rows]], 0).T
        s = swap(x)
        low = low_half(x.shape)
        pr, pi = jnp.where(low, x, s), jnp.where(low, -s, x)
        pr_ref[rows, :] = pr
        pi_ref[rows, :] = pi
        w = wide_ref[pl.ds(off + start, 128), :]
        win_ref[rows, :] = w.astype(BF16)
        x_ref[rows, :] = (w * pr + swap(w) * pi).astype(BF16).astype(F32)
    dft(x_ref, t_ref, g_ref, 1, store_rows(x_ref))
    turn_blocks(x_ref, out_ref)


def middle_kernel(recv_ref, intensity_ref, t_ref, out_ref, root_ref, x_ref, g_ref):
    x_ref[...] = recv_ref[...].astype(F32)
    for start in range(0, W, 128):
        rows = slice(start, start + 128)
        root = jnp.sqrt(intensity_ref[0, :, rows])
        root_ref[rows, :] = jnp.concatenate([root, root], 0).T

    def replace(start, value):
        squared = value * value
        magnitude = jnp.sqrt(squared + swap(squared))
        rows = slice(start, start + value.shape[0])
        scaling = root_ref[rows, :] / jnp.maximum(magnitude, AMPLITUDE_FLOOR)
        x_ref[rows, :] = (value * scaling).astype(BF16).astype(F32)

    dft(x_ref, t_ref, g_ref, 1, replace)
    dft(x_ref, t_ref, g_ref, -1, store_rows(x_ref))
    turn_blocks(x_ref, out_ref)


def last_kernel(row_ref, recv_ref, win_ref, pr_ref, pi_ref, t_ref, grad_ref, corr_ref, x_ref, c_ref, g_ref):
    row = row_ref[lax.axis_index("led")]
    x_ref[...] = recv_ref[...].astype(F32)

    def update(start, estimate):
        size = estimate.shape[0]
        rows = slice(start, start + size)
        w = win_ref[rows, :].astype(F32)
        pr, pi = pr_ref[rows, :], pi_ref[rows, :]
        ws = swap(w)
        low = low_half(w.shape)
        change = estimate - (w * pr + ws * pi)
        cs = swap(change)
        wr = jnp.where(low, w, ws)
        wi = jnp.where(low, ws, -w)
        grad_ref[rows, :] = (change * wr + cs * wi).astype(BF16)
        c_ref[pl.ds(row + start, size), :] = (change * pr - cs * pi) / (pr * pr + pi * pi + PUPIL_DAMPING)

    dft(x_ref, t_ref, g_ref, -1, update)

    for part in range(32):
        start = part * 64
        classes = start + lax.broadcasted_iota(jnp.int32, (64, 128), 0)
        value = jnp.where(classes < row, c_ref[start + W : start + W + 64, :], c_ref[start : start + 64, :])
        dest = (part % 2) * 16 + part // 2
        corr_ref[dest * 64 : dest * 64 + 64, :] = value.astype(BF16)


def reduce_kernel(row_ref, col_ref, recv_ref, own_ref, other_ref, acc_ref):
    slab, led = lax.axis_index("slab"), lax.axis_index("led")
    upper = slab // 16
    base = (slab % 16) * 128 + upper * 64 + led * 8
    acc_ref[...] = jnp.zeros_like(acc_ref)
    lanes = lax.broadcasted_iota(jnp.int32, (16, 128), 1)
    low = lax.broadcasted_iota(jnp.int32, (8, 128), 1) < BAND
    classes = base + lax.rem(lax.broadcasted_iota(jnp.int32, (16, 128), 0), 8)

    def pair(p, carry):
        for j in range(2):
            row, col = row_ref[2 * p + j], col_ref[2 * p + j]
            tile = col // 128
            lo = col - tile * 128
            take = lanes >= lo
            mine = (classes < row) == (upper == 1)

            def put(t, value):
                rows = pl.ds(pl.multiple_of((tile + t) * 16, 16), 16)
                acc_ref[0, rows, :] += jnp.where(mine, value, 0.0)
                acc_ref[1, rows, :] += jnp.where(mine, 0.0, value)

            last = jnp.zeros((16, 128), F32)
            for t in range(W // 128):
                at = pl.multiple_of(t * 128 + p * 16, 16)
                x = recv_ref[pl.ds(at, 16), :].astype(F32)[8 * j : 8 * j + 8]
                y = recv_ref[pl.ds(pl.multiple_of(at + 64, 16), 16), :].astype(F32)[8 * j : 8 * j + 8]
                both = jnp.concatenate([jnp.where(low, x, swap(y)), jnp.where(low, swap(x), y)], 0)
                both = pltpu.roll(both, lo, 1)
                put(t, jnp.where(take, both, last))
                last = both
            put(W // 128, jnp.where(take, 0.0, last))
        return carry

    lax.fori_loop(0, 4, pair, 0)
    own_ref[...] = acc_ref[0, : NC // 8, :].astype(BF16)
    other_ref[...] = acc_ref[1, : NC // 8, :].astype(BF16)


def merge_kernel(grad_ref, swapped_ref, *refs):
    out_ref = refs[-1]
    out_ref[: NC // 8, :] = swapped_ref[...]
    for start in range(0, W // 8, 64):
        total = grad_ref[start : start + 64, :].astype(F32)
        for j in range(1, 8):
            total += grad_ref[j * (W // 8) + start : j * (W // 8) + start + 64, :].astype(F32)
        out_ref[NC // 8 + start : NC // 8 + start + 64, :] = total.astype(BF16)


HOPS = (0, 1, -1, 2, -2, 3, -3, 4)


def finish_kernel(hops, *refs):
    n = len(hops)
    spec_ref, own, rest = refs[0], refs[1 : n + 1], refs[n + 1 : 2 * n + 1]
    new_ref, out_ref, sum_ref, turn_ref, sum_sem, turn_sem = refs[-6:]
    slab, led = lax.axis_index("slab"), lax.axis_index("led")
    upper = slab // 16
    copies = []
    for i, hop in enumerate(hops):
        source = lax.rem(led - hop + 8, 8)
        for part, half, ref in ((0, upper, own[i]), (1, 1 - upper, rest[i])):
            rows = pl.ds(pl.multiple_of(half * 64 + source * 8, 8), 8)
            for t in range(NC // 128):
                x = ref[t * 16 : t * 16 + 16, :].astype(F32)
                columns = slice(t * 128, t * 128 + 128)
                sum_ref[2 * i + part, 0, :, columns] = spec_ref[0, rows, columns] + x[:8]
                sum_ref[2 * i + part, 1, :, columns] = spec_ref[1, rows, columns] + x[8:]
            copies.append(
                pltpu.make_async_copy(sum_ref.at[2 * i + part], new_ref.at[:, rows, :], sum_sem.at[2 * i + part])
            )
            copies[-1].start()
        for t in range(2):
            start = NC // 8 + t * 128
            x = rest[i][start : start + 128, :].astype(F32).T
            turn_ref[i, 0, :, t * 128 : t * 128 + 128] = x[:BAND]
            turn_ref[i, 1, :, t * 128 : t * 128 + 128] = x[BAND:]
        columns = pl.ds(pl.multiple_of(source * 256, 256), 256)
        copies.append(pltpu.make_async_copy(turn_ref.at[i], out_ref.at[:, :, columns], turn_sem.at[i]))
        copies[-1].start()
    for copy in copies:
        copy.wait()


def finish(hops, spectrum, own, rest, before=()):
    n = len(hops)
    shapes = [jax.ShapeDtypeStruct((2, 128, NC), F32), jax.ShapeDtypeStruct((2, BAND, W), F32)]
    return pl.pallas_call(
        functools.partial(finish_kernel, hops),
        out_shape=shapes,
        in_specs=[pl.BlockSpec(memory_space=VMEM)] * (2 * n + 1) + [pl.BlockSpec(memory_space=pl.ANY)] * len(before),
        out_specs=[pl.BlockSpec(memory_space=pl.ANY)] * 2,
        input_output_aliases={2 * n + 1 + i: i for i in range(len(before))},
        scratch_shapes=[
            VMEM((2 * n, 2, 8, NC), F32),
            VMEM((n, 2, BAND, W // 8), F32),
            pltpu.SemaphoreType.DMA((2 * n,)),
            pltpu.SemaphoreType.DMA((n,)),
        ],
        compiler_params=pltpu.CompilerParams(vmem_limit_bytes=20 * MIB),
        cost_estimate=pl.CostEstimate(flops=0, bytes_accessed=n * 2 * MIB, transcendentals=0),
    )(spectrum, *own, *rest, *before)


def call(kernel, outs, scalars, arrays, scratch=(), flops=0, limit=20 * MIB):
    shapes = [jax.ShapeDtypeStruct(s, d) for s, d in outs]
    moved = sum(math.prod(s) * jnp.dtype(d).itemsize for s, d in outs)
    moved += sum(a.size * a.dtype.itemsize for a in arrays)
    return pl.pallas_call(
        kernel,
        out_shape=shapes,
        in_specs=[pl.BlockSpec(memory_space=pltpu.SMEM)] * len(scalars)
        + [pl.BlockSpec(memory_space=VMEM)] * len(arrays),
        out_specs=[pl.BlockSpec(memory_space=VMEM)] * len(outs),
        scratch_shapes=list(scratch),
        compiler_params=pltpu.CompilerParams(vmem_limit_bytes=limit),
        cost_estimate=pl.CostEstimate(flops=flops, bytes_accessed=moved, transcendentals=0),
    )(*scalars, *arrays)


def turn_bands(values):
    blocks = values.reshape(32, -1, 128)
    return lax.all_to_all(blocks, "slab", 0, 0).reshape(-1, 128)


FORWARD = [(i, (i + 1) % 8) for i in range(8)]
BACKWARD = [(i, (i - 1) % 8) for i in range(8)]


def ring_gather(piece):
    forward = backward = piece
    found = [piece]
    for hop in range(1, 5):
        forward = lax.ppermute(forward, "led", FORWARD)
        found.append(forward)
        if hop < 4:
            backward = lax.ppermute(backward, "led", BACKWARD)
            found.append(backward)
    return found


def per_device(spectrum, pupil, intensity, row_offsets, col_offsets):
    tab = jnp.asarray(table())
    rows128 = (W, 128)
    flops = 8 * QUARTER * 1024 * 128

    (outgoing,) = call(
        gather_kernel, [((2 * W, 128), BF16)], [col_offsets], [spectrum], [VMEM((2, 128, W + 128), BF16)]
    )
    arrived = turn_bands(outgoing)
    scratch = [VMEM(rows128, F32), VMEM((4, QUARTER, 128), F32)]
    first, window, pr, pi = call(
        first_kernel,
        [(rows128, BF16), (rows128, BF16), (rows128, F32), (rows128, F32)],
        [row_offsets],
        [arrived, pupil, tab],
        [VMEM((W + 16, 128), F32)] + scratch,
        flops,
    )
    turned = turn_bands(first)
    (second,) = call(
        middle_kernel, [(rows128, BF16)], [], [turned, intensity, tab], [VMEM(rows128, F32)] + scratch, 2 * flops
    )
    returned = turn_bands(second)
    gradient, correction = call(
        last_kernel,
        [(rows128, BF16), (rows128, BF16)],
        [row_offsets],
        [returned, window, pr, pi, tab],
        [VMEM(rows128, F32), VMEM((2 * W, 128), F32), VMEM((4, QUARTER, 128), F32)],
        flops,
    )
    landed = lax.all_to_all(correction.reshape(256, 8, 128), ("slab", "led"), 0, 0).reshape(rows128)
    gradient, landed = lax.optimization_barrier((gradient, landed))
    piece = NC // 8
    own, other = call(
        reduce_kernel,
        [((piece, 128), BF16)] * 2,
        [row_offsets, col_offsets],
        [landed],
        [VMEM((2, piece + 16, 128), F32)],
    )
    swapped = lax.ppermute(other, "slab", [(i, (i + 16) % 32) for i in range(32)])
    grads = lax.all_to_all(gradient.reshape(8, W // 8, 128), "led", 0, 0).reshape(rows128)
    own_pieces = ring_gather(own)
    (rest,) = call(merge_kernel, [((piece + W // 8, 128), BF16)], [], [grads, swapped, *own_pieces[1:3]])
    rest_pieces = ring_gather(rest)
    near = finish(HOPS[:7], spectrum, own_pieces[:7], rest_pieces[:7])
    return finish(HOPS[7:], spectrum, own_pieces[7:], rest_pieces[7:], near)


def solution(mesh):
    in_specs = (P(None, "slab", None), P(None, "slab", None), P("led", "slab", None), P(), P())
    out_specs = (P(None, "slab", None), P(None, "slab", None))
    return jax.shard_map(per_device, mesh=mesh, in_specs=in_specs, out_specs=out_specs, check_vma=False)
```

```python
import functools
import math

import jax
import jax.numpy as jnp
import numpy as np
from jax import lax
from jax.experimental import pallas as pl
from jax.experimental.pallas import tpu as pltpu
from jax.sharding import PartitionSpec as P

W = 2048
QUARTER = W // 4
BAND = 64
NC = 3072
AMPLITUDE_FLOOR = 0.5
PUPIL_DAMPING = 0.5
MIB = 1024 * 1024

VMEM = pltpu.VMEM
F32 = jnp.float32
BF16 = jnp.bfloat16


def table():
    rows = np.arange(QUARTER, dtype=np.int64)[:, None]
    cols = np.arange(W, dtype=np.int64)[None, :]
    phases = ((rows * cols) % W).astype(np.float32) * np.float32(2.0 * math.pi / W)
    factor = np.float32(1.0 / math.sqrt(W))
    parts = []
    for res in range(4):
        part = phases[:, res::4]
        parts.append(np.concatenate([np.cos(part) * factor, np.sin(part) * factor], 1))
    return np.stack(parts).astype(jnp.bfloat16)


def low_half(shape):
    return lax.broadcasted_iota(jnp.int32, shape, 1) < BAND


def swap(x):
    return pltpu.roll(x, BAND, 1)


def times_i(x):
    s = swap(x)
    return jnp.where(low_half(x.shape), -s, s)


def dft(x_ref, t_ref, g_ref, sign, emit, chunk=64):
    for res in range(4):
        x = x_ref[pl.ds(res, QUARTER, stride=4), :]
        ix = times_i(x)
        if sign < 0:
            ix = -ix
        operand = jnp.concatenate([x.astype(BF16), ix.astype(BF16)], 0)
        g_ref[res] = jnp.dot(t_ref[res], operand, preferred_element_type=F32)

    for start in range(0, QUARTER, chunk):
        g0, g1, g2, g3 = (g_ref[res, start : start + chunk, :] for res in range(4))
        h0, h1, h2 = g0 + g2, g0 - g2, g1 + g3
        h3 = times_i(g1 - g3)
        if sign < 0:
            h3 = -h3
        emit(start, h0 + h2)
        emit(QUARTER + start, h1 + h3)
        emit(2 * QUARTER + start, h0 - h2)
        emit(3 * QUARTER + start, h1 - h3)


def store_rows(ref):
    def emit(start, value):
        ref[start : start + value.shape[0], :] = value

    return emit


def turn_blocks(x_ref, out_ref):
    for base in range(0, W, 128):
        turned = x_ref[base : base + 128, :].T
        a, b = turned[:BAND], turned[BAND:]
        low = low_half(a.shape)
        out_ref[base : base + BAND, :] = jnp.where(low, a, swap(b)).astype(BF16)
        out_ref[base + BAND : base + 128, :] = jnp.where(low, swap(a), b).astype(BF16)


def gather_kernel(col_ref, spec_ref, out_ref, x_ref):
    col = col_ref[lax.axis_index("led")]
    tile = col // 128
    lo = col - tile * 128
    for t in range(W // 128 + 1):
        source = jnp.minimum(tile + t, NC // 128 - 1)
        x_ref[:, :, t * 128 : t * 128 + 128] = spec_ref[:, :, pl.ds(pl.multiple_of(source * 128, 128), 128)].astype(BF16)
    source = lax.broadcasted_iota(jnp.int32, (512, 256), 0)
    target = lax.broadcasted_iota(jnp.int32, (512, 256), 1)
    moves = (source % 256 == lo + target // 128 * 64 + target % 64) & (source // 256 == target % 128 // 64)
    moves = moves.astype(F32).astype(BF16)
    for t in range(W // 128):
        columns = slice(t * 128, t * 128 + 256)
        both = jnp.concatenate([x_ref[0, :, columns], x_ref[1, :, columns]], 1)
        moved = jnp.dot(both, moves, preferred_element_type=F32)
        out_ref[t * 256 : t * 256 + 128, :] = moved[:, :128].astype(BF16)
        out_ref[t * 256 + 128 : t * 256 + 256, :] = moved[:, 128:].astype(BF16)


def first_kernel(row_ref, recv_ref, pupil_ref, t_ref, out_ref, win_ref, pr_ref, pi_ref, wide_ref, x_ref, g_ref):
    row = row_ref[lax.axis_index("led")]
    base = jnp.minimum(row // 16 * 16, 2 * W - (W + 16))
    off = row - base
    wide_ref[...] = recv_ref[pl.ds(pl.multiple_of(base, 16), W + 16), :].astype(F32)
    for start in range(0, W, 128):
        rows = slice(start, start + 128)
        x = jnp.concatenate([pupil_ref[0, :, rows], pupil_ref[1, :, rows]], 0).T
        s = swap(x)
        low = low_half(x.shape)
        pr, pi = jnp.where(low, x, s), jnp.where(low, -s, x)
        pr_ref[rows, :] = pr
        pi_ref[rows, :] = pi
        w = wide_ref[pl.ds(off + start, 128), :]
        win_ref[rows, :] = w.astype(BF16)
        x_ref[rows, :] = (w * pr + swap(w) * pi).astype(BF16).astype(F32)
    dft(x_ref, t_ref, g_ref, 1, store_rows(x_ref))
    turn_blocks(x_ref, out_ref)


def middle_kernel(recv_ref, intensity_ref, t_ref, out_ref, root_ref, x_ref, g_ref):
    x_ref[...] = recv_ref[...].astype(F32)
    for start in range(0, W, 128):
        rows = slice(start, start + 128)
        root = jnp.sqrt(intensity_ref[0, :, rows])
        root_ref[rows, :] = jnp.concatenate([root, root], 0).T

    def replace(start, value):
        squared = value * value
        magnitude = jnp.sqrt(squared + swap(squared))
        rows = slice(start, start + value.shape[0])
        scaling = root_ref[rows, :] / jnp.maximum(magnitude, AMPLITUDE_FLOOR)
        x_ref[rows, :] = (value * scaling).astype(BF16).astype(F32)

    dft(x_ref, t_ref, g_ref, 1, replace)
    dft(x_ref, t_ref, g_ref, -1, store_rows(x_ref))
    turn_blocks(x_ref, out_ref)


def last_kernel(row_ref, recv_ref, win_ref, pr_ref, pi_ref, t_ref, grad_ref, corr_ref, x_ref, c_ref, g_ref):
    row = row_ref[lax.axis_index("led")]
    x_ref[...] = recv_ref[...].astype(F32)

    def update(start, estimate):
        size = estimate.shape[0]
        rows = slice(start, start + size)
        w = win_ref[rows, :].astype(F32)
        pr, pi = pr_ref[rows, :], pi_ref[rows, :]
        ws = swap(w)
        low = low_half(w.shape)
        change = estimate - (w * pr + ws * pi)
        cs = swap(change)
        wr = jnp.where(low, w, ws)
        wi = jnp.where(low, ws, -w)
        grad_ref[rows, :] = (change * wr + cs * wi).astype(BF16)
        c_ref[pl.ds(row + start, size), :] = (change * pr - cs * pi) / (pr * pr + pi * pi + PUPIL_DAMPING)

    dft(x_ref, t_ref, g_ref, -1, update)

    for part in range(32):
        start = part * 64
        classes = start + lax.broadcasted_iota(jnp.int32, (64, 128), 0)
        value = jnp.where(classes < row, c_ref[start + W : start + W + 64, :], c_ref[start : start + 64, :])
        dest = (part % 2) * 16 + part // 2
        corr_ref[dest * 64 : dest * 64 + 64, :] = value.astype(BF16)


def reduce_kernel(row_ref, col_ref, recv_ref, own_ref, other_ref, acc_ref):
    slab, led = lax.axis_index("slab"), lax.axis_index("led")
    upper = slab // 16
    base = (slab % 16) * 128 + upper * 64 + led * 8
    acc_ref[...] = jnp.zeros_like(acc_ref)
    lanes = lax.broadcasted_iota(jnp.int32, (16, 128), 1)
    low = lax.broadcasted_iota(jnp.int32, (8, 128), 1) < BAND
    classes = base + lax.rem(lax.broadcasted_iota(jnp.int32, (16, 128), 0), 8)

    def pair(p, carry):
        for j in range(2):
            row, col = row_ref[2 * p + j], col_ref[2 * p + j]
            tile = col // 128
            lo = col - tile * 128
            take = lanes >= lo
            mine = (classes < row) == (upper == 1)

            def put(t, value):
                rows = pl.ds(pl.multiple_of((tile + t) * 16, 16), 16)
                acc_ref[0, rows, :] += jnp.where(mine, value, 0.0)
                acc_ref[1, rows, :] += jnp.where(mine, 0.0, value)

            last = jnp.zeros((16, 128), F32)
            for t in range(W // 128):
                at = pl.multiple_of(t * 128 + p * 16, 16)
                x = recv_ref[pl.ds(at, 16), :].astype(F32)[8 * j : 8 * j + 8]
                y = recv_ref[pl.ds(pl.multiple_of(at + 64, 16), 16), :].astype(F32)[8 * j : 8 * j + 8]
                both = jnp.concatenate([jnp.where(low, x, swap(y)), jnp.where(low, swap(x), y)], 0)
                both = pltpu.roll(both, lo, 1)
                put(t, jnp.where(take, both, last))
                last = both
            put(W // 128, jnp.where(take, 0.0, last))
        return carry

    lax.fori_loop(0, 4, pair, 0)
    own_ref[...] = acc_ref[0, : NC // 8, :].astype(BF16)
    other_ref[...] = acc_ref[1, : NC // 8, :].astype(BF16)


def merge_kernel(grad_ref, swapped_ref, *refs):
    out_ref = refs[-1]
    out_ref[: NC // 8, :] = swapped_ref[...]
    for start in range(0, W // 8, 64):
        total = grad_ref[start : start + 64, :].astype(F32)
        for j in range(1, 8):
            total += grad_ref[j * (W // 8) + start : j * (W // 8) + start + 64, :].astype(F32)
        out_ref[NC // 8 + start : NC // 8 + start + 64, :] = total.astype(BF16)


HOPS = (0, 1, -1, 2, -2, 3, -3, 4)


def finish_kernel(hops, *refs):
    n = len(hops)
    spec_ref, own, rest = refs[0], refs[1 : n + 1], refs[n + 1 : 2 * n + 1]
    new_ref, out_ref, sum_ref, turn_ref, sum_sem, turn_sem = refs[-6:]
    slab, led = lax.axis_index("slab"), lax.axis_index("led")
    upper = slab // 16
    copies = []
    for i, hop in enumerate(hops):
        source = lax.rem(led - hop + 8, 8)
        for part, half, ref in ((0, upper, own[i]), (1, 1 - upper, rest[i])):
            rows = pl.ds(pl.multiple_of(half * 64 + source * 8, 8), 8)
            for t in range(NC // 128):
                x = ref[t * 16 : t * 16 + 16, :].astype(F32)
                columns = slice(t * 128, t * 128 + 128)
                sum_ref[2 * i + part, 0, :, columns] = spec_ref[0, rows, columns] + x[:8]
                sum_ref[2 * i + part, 1, :, columns] = spec_ref[1, rows, columns] + x[8:]
            copies.append(
                pltpu.make_async_copy(sum_ref.at[2 * i + part], new_ref.at[:, rows, :], sum_sem.at[2 * i + part])
            )
            copies[-1].start()
        for t in range(2):
            start = NC // 8 + t * 128
            x = rest[i][start : start + 128, :].astype(F32).T
            turn_ref[i, 0, :, t * 128 : t * 128 + 128] = x[:BAND]
            turn_ref[i, 1, :, t * 128 : t * 128 + 128] = x[BAND:]
        columns = pl.ds(pl.multiple_of(source * 256, 256), 256)
        copies.append(pltpu.make_async_copy(turn_ref.at[i], out_ref.at[:, :, columns], turn_sem.at[i]))
        copies[-1].start()
    for copy in copies:
        copy.wait()


def finish(hops, spectrum, own, rest, before=()):
    n = len(hops)
    shapes = [jax.ShapeDtypeStruct((2, 128, NC), F32), jax.ShapeDtypeStruct((2, BAND, W), F32)]
    return pl.pallas_call(
        functools.partial(finish_kernel, hops),
        out_shape=shapes,
        in_specs=[pl.BlockSpec(memory_space=VMEM)] * (2 * n + 1) + [pl.BlockSpec(memory_space=pl.ANY)] * len(before),
        out_specs=[pl.BlockSpec(memory_space=pl.ANY)] * 2,
        input_output_aliases={2 * n + 1 + i: i for i in range(len(before))},
        scratch_shapes=[
            VMEM((2 * n, 2, 8, NC), F32),
            VMEM((n, 2, BAND, W // 8), F32),
            pltpu.SemaphoreType.DMA((2 * n,)),
            pltpu.SemaphoreType.DMA((n,)),
        ],
        compiler_params=pltpu.CompilerParams(vmem_limit_bytes=20 * MIB),
        cost_estimate=pl.CostEstimate(flops=0, bytes_accessed=n * 2 * MIB, transcendentals=0),
    )(spectrum, *own, *rest, *before)


def call(kernel, outs, scalars, arrays, scratch=(), flops=0, limit=20 * MIB):
    shapes = [jax.ShapeDtypeStruct(s, d) for s, d in outs]
    moved = sum(math.prod(s) * jnp.dtype(d).itemsize for s, d in outs)
    moved += sum(a.size * a.dtype.itemsize for a in arrays)
    return pl.pallas_call(
        kernel,
        out_shape=shapes,
        in_specs=[pl.BlockSpec(memory_space=pltpu.SMEM)] * len(scalars)
        + [pl.BlockSpec(memory_space=VMEM)] * len(arrays),
        out_specs=[pl.BlockSpec(memory_space=VMEM)] * len(outs),
        scratch_shapes=list(scratch),
        compiler_params=pltpu.CompilerParams(vmem_limit_bytes=limit),
        cost_estimate=pl.CostEstimate(flops=flops, bytes_accessed=moved, transcendentals=0),
    )(*scalars, *arrays)


def turn_bands(values):
    blocks = values.reshape(32, -1, 128)
    return lax.all_to_all(blocks, "slab", 0, 0).reshape(-1, 128)


FORWARD = [(i, (i + 1) % 8) for i in range(8)]
BACKWARD = [(i, (i - 1) % 8) for i in range(8)]


def ring_gather(piece, before=None):
    up = down = piece
    found = [piece]
    for hop in range(1, 5):
        if before is not None and hop == 2:
            up, down = lax.optimization_barrier((up, down, *before[3:5]))[:2]
        up = lax.ppermute(up, "led", FORWARD)
        found.append(up)
        if hop < 4:
            down = lax.ppermute(down, "led", BACKWARD)
            found.append(down)
    return found


def per_device(spectrum, pupil, intensity, row_offsets, col_offsets):
    tab = jnp.asarray(table())
    rows128 = (W, 128)
    flops = 8 * QUARTER * 1024 * 128

    (outgoing,) = call(
        gather_kernel, [((2 * W, 128), BF16)], [col_offsets], [spectrum], [VMEM((2, 128, W + 128), BF16)]
    )
    arrived = turn_bands(outgoing)
    scratch = [VMEM(rows128, F32), VMEM((4, QUARTER, 128), F32)]
    first, window, pr, pi = call(
        first_kernel,
        [(rows128, BF16), (rows128, BF16), (rows128, F32), (rows128, F32)],
        [row_offsets],
        [arrived, pupil, tab],
        [VMEM((W + 16, 128), F32)] + scratch,
        flops,
    )
    turned = turn_bands(first)
    (second,) = call(
        middle_kernel, [(rows128, BF16)], [], [turned, intensity, tab], [VMEM(rows128, F32)] + scratch, 2 * flops
    )
    returned = turn_bands(second)
    gradient, correction = call(
        last_kernel,
        [(rows128, BF16), (rows128, BF16)],
        [row_offsets],
        [returned, window, pr, pi, tab],
        [VMEM(rows128, F32), VMEM((2 * W, 128), F32), VMEM((4, QUARTER, 128), F32)],
        flops,
    )
    landed = lax.all_to_all(correction.reshape(256, 8, 128), ("slab", "led"), 0, 0).reshape(rows128)
    gradient, landed = lax.optimization_barrier((gradient, landed))
    piece = NC // 8
    own, other = call(
        reduce_kernel,
        [((piece, 128), BF16)] * 2,
        [row_offsets, col_offsets],
        [landed],
        [VMEM((2, piece + 16, 128), F32)],
    )
    swapped = lax.ppermute(other, "slab", [(i, (i + 16) % 32) for i in range(32)])
    grads = lax.all_to_all(gradient.reshape(8, W // 8, 128), "led", 0, 0).reshape(rows128)
    own_pieces = ring_gather(own)
    (rest,) = call(merge_kernel, [((piece + W // 8, 128), BF16)], [], [grads, swapped, *own_pieces[1:3]])
    rest_pieces = ring_gather(rest, own_pieces)
    near = finish(HOPS[:7], spectrum, own_pieces[:7], rest_pieces[:7])
    return finish(HOPS[7:], spectrum, own_pieces[7:], rest_pieces[7:], near)


def solution(mesh):
    in_specs = (P(None, "slab", None), P(None, "slab", None), P("led", "slab", None), P(), P())
    out_specs = (P(None, "slab", None), P(None, "slab", None))
    return jax.shard_map(per_device, mesh=mesh, in_specs=in_specs, out_specs=out_specs, check_vma=False)
```

```python
import functools
import math

import jax
import jax.numpy as jnp
import numpy as np
from jax import lax
from jax.experimental import pallas as pl
from jax.experimental.pallas import tpu as pltpu
from jax.sharding import PartitionSpec as P

W = 2048
QUARTER = W // 4
BAND = 64
NC = 3072
AMPLITUDE_FLOOR = 0.5
PUPIL_DAMPING = 0.5
MIB = 1024 * 1024

VMEM = pltpu.VMEM
F32 = jnp.float32
BF16 = jnp.bfloat16


def tables():
    rows = np.arange(QUARTER, dtype=np.int64)[:, None]
    columns = 4 * np.arange(QUARTER, dtype=np.int64)[None, :]
    phases = ((rows * columns) % W).astype(np.float32) * np.float32(2.0 * math.pi / W)
    factor = np.float32(1.0 / math.sqrt(W))
    base = np.concatenate([np.cos(phases) * factor, np.sin(phases) * factor], 1).astype(jnp.bfloat16)
    turns = []
    for res in range(1, 4):
        angle = rows * res * (2.0 * math.pi / W)
        ones = np.ones((1, BAND))
        low, high = np.concatenate([ones, 0 * ones], 1), np.concatenate([0 * ones, ones], 1)
        turns.append([np.cos(angle) * (low + high), np.sin(angle) * (high - low)])
    return base, np.array(turns, np.float32)


def low_half(shape):
    return lax.broadcasted_iota(jnp.int32, shape, 1) < BAND


def swap(x):
    return pltpu.roll(x, BAND, 1)


def times_i(x):
    s = swap(x)
    return jnp.where(low_half(x.shape), -s, s)


def dft(x_ref, t_ref, w_ref, g_ref, sign, emit, chunk=64):
    operands = []
    for res in range(4):
        x = x_ref[pl.ds(res, QUARTER, stride=4), :]
        ix = times_i(x)
        if sign < 0:
            ix = -ix
        operands.append(jnp.concatenate([x.astype(BF16), ix.astype(BF16)], 0))
    for half in range(2):
        operand = jnp.concatenate(operands[2 * half : 2 * half + 2], 1)
        g_ref[:, half * 256 : half * 256 + 256] = jnp.dot(t_ref[...], operand, preferred_element_type=F32)

    for start in range(0, QUARTER, chunk):
        rows = slice(start, start + chunk)
        g0 = g_ref[rows, :128]
        turned = []
        for res in range(1, 4):
            g = g_ref[rows, res * 128 : res * 128 + 128]
            imaginary = swap(g) * w_ref[res - 1, 1, rows, :]
            g = g * w_ref[res - 1, 0, rows, :]
            turned.append(g + imaginary if sign > 0 else g - imaginary)
        g1, g2, g3 = turned
        h0, h1, h2 = g0 + g2, g0 - g2, g1 + g3
        h3 = times_i(g1 - g3)
        if sign < 0:
            h3 = -h3
        emit(start, h0 + h2)
        emit(QUARTER + start, h1 + h3)
        emit(2 * QUARTER + start, h0 - h2)
        emit(3 * QUARTER + start, h1 - h3)


def store_rows(ref):
    def emit(start, value):
        ref[start : start + value.shape[0], :] = value

    return emit


def turn_blocks(x_ref, out_ref):
    for base in range(0, W, 128):
        turned = x_ref[base : base + 128, :].T
        a, b = turned[:BAND], turned[BAND:]
        low = low_half(a.shape)
        out_ref[base : base + BAND, :] = jnp.where(low, a, swap(b)).astype(BF16)
        out_ref[base + BAND : base + 128, :] = jnp.where(low, swap(a), b).astype(BF16)


def gather_kernel(col_ref, spec_ref, out_ref, x_ref):
    col = col_ref[lax.axis_index("led")]
    tile = col // 128
    lo = col - tile * 128
    for t in range(W // 128 + 1):
        source = jnp.minimum(tile + t, NC // 128 - 1)
        x_ref[:, :, t * 128 : t * 128 + 128] = spec_ref[:, :, pl.ds(pl.multiple_of(source * 128, 128), 128)].astype(BF16)
    source = lax.broadcasted_iota(jnp.int32, (512, 256), 0)
    target = lax.broadcasted_iota(jnp.int32, (512, 256), 1)
    moves = (source % 256 == lo + target // 128 * 64 + target % 64) & (source // 256 == target % 128 // 64)
    moves = moves.astype(F32).astype(BF16)
    for t in range(W // 128):
        columns = slice(t * 128, t * 128 + 256)
        both = jnp.concatenate([x_ref[0, :, columns], x_ref[1, :, columns]], 1)
        moved = jnp.dot(both, moves, preferred_element_type=F32)
        out_ref[t * 256 : t * 256 + 128, :] = moved[:, :128].astype(BF16)
        out_ref[t * 256 + 128 : t * 256 + 256, :] = moved[:, 128:].astype(BF16)


def first_kernel(row_ref, recv_ref, pupil_ref, t_ref, w_ref, out_ref, win_ref, pr_ref, pi_ref, wide_ref, x_ref, g_ref):
    row = row_ref[lax.axis_index("led")]
    base = jnp.minimum(row // 16 * 16, 2 * W - (W + 16))
    off = row - base
    wide_ref[...] = recv_ref[pl.ds(pl.multiple_of(base, 16), W + 16), :].astype(F32)
    for start in range(0, W, 128):
        rows = slice(start, start + 128)
        x = jnp.concatenate([pupil_ref[0, :, rows], pupil_ref[1, :, rows]], 0).T
        s = swap(x)
        low = low_half(x.shape)
        pr, pi = jnp.where(low, x, s), jnp.where(low, -s, x)
        pr_ref[rows, :] = pr
        pi_ref[rows, :] = pi
        w = wide_ref[pl.ds(off + start, 128), :]
        win_ref[rows, :] = w.astype(BF16)
        x_ref[rows, :] = (w * pr + swap(w) * pi).astype(BF16).astype(F32)
    dft(x_ref, t_ref, w_ref, g_ref, 1, store_rows(x_ref))
    turn_blocks(x_ref, out_ref)


def middle_kernel(recv_ref, intensity_ref, t_ref, w_ref, out_ref, root_ref, x_ref, g_ref):
    x_ref[...] = recv_ref[...].astype(F32)
    for start in range(0, W, 128):
        rows = slice(start, start + 128)
        root = jnp.sqrt(intensity_ref[0, :, rows])
        root_ref[rows, :] = jnp.concatenate([root, root], 0).T

    def replace(start, value):
        squared = value * value
        magnitude = jnp.sqrt(squared + swap(squared))
        rows = slice(start, start + value.shape[0])
        scaling = root_ref[rows, :] / jnp.maximum(magnitude, AMPLITUDE_FLOOR)
        x_ref[rows, :] = (value * scaling).astype(BF16).astype(F32)

    dft(x_ref, t_ref, w_ref, g_ref, 1, replace)
    dft(x_ref, t_ref, w_ref, g_ref, -1, store_rows(x_ref))
    turn_blocks(x_ref, out_ref)


def last_kernel(row_ref, recv_ref, win_ref, pr_ref, pi_ref, t_ref, w_ref, grad_ref, corr_ref, x_ref, c_ref, g_ref):
    row = row_ref[lax.axis_index("led")]
    x_ref[...] = recv_ref[...].astype(F32)

    def update(start, estimate):
        size = estimate.shape[0]
        rows = slice(start, start + size)
        w = win_ref[rows, :].astype(F32)
        pr, pi = pr_ref[rows, :], pi_ref[rows, :]
        ws = swap(w)
        low = low_half(w.shape)
        change = estimate - (w * pr + ws * pi)
        cs = swap(change)
        wr = jnp.where(low, w, ws)
        wi = jnp.where(low, ws, -w)
        grad_ref[rows, :] = (change * wr + cs * wi).astype(BF16)
        c_ref[pl.ds(row + start, size), :] = (change * pr - cs * pi) / (pr * pr + pi * pi + PUPIL_DAMPING)

    dft(x_ref, t_ref, w_ref, g_ref, -1, update)

    for part in range(32):
        start = part * 64
        classes = start + lax.broadcasted_iota(jnp.int32, (64, 128), 0)
        value = jnp.where(classes < row, c_ref[start + W : start + W + 64, :], c_ref[start : start + 64, :])
        dest = (part % 2) * 16 + part // 2
        corr_ref[dest * 64 : dest * 64 + 64, :] = value.astype(BF16)


def reduce_kernel(row_ref, col_ref, recv_ref, own_ref, other_ref, acc_ref):
    slab, led = lax.axis_index("slab"), lax.axis_index("led")
    upper = slab // 16
    base = (slab % 16) * 128 + upper * 64 + led * 8
    acc_ref[...] = jnp.zeros_like(acc_ref)
    lanes = lax.broadcasted_iota(jnp.int32, (16, 128), 1)
    low = lax.broadcasted_iota(jnp.int32, (8, 128), 1) < BAND
    classes = base + lax.rem(lax.broadcasted_iota(jnp.int32, (16, 128), 0), 8)

    def pair(p, carry):
        for j in range(2):
            row, col = row_ref[2 * p + j], col_ref[2 * p + j]
            tile = col // 128
            lo = col - tile * 128
            take = lanes >= lo
            mine = (classes < row) == (upper == 1)

            def put(t, value):
                rows = pl.ds(pl.multiple_of((tile + t) * 16, 16), 16)
                acc_ref[0, rows, :] += jnp.where(mine, value, 0.0)
                acc_ref[1, rows, :] += jnp.where(mine, 0.0, value)

            last = jnp.zeros((16, 128), F32)
            for t in range(W // 128):
                at = pl.multiple_of(t * 128 + p * 16, 16)
                x = recv_ref[pl.ds(at, 16), :].astype(F32)[8 * j : 8 * j + 8]
                y = recv_ref[pl.ds(pl.multiple_of(at + 64, 16), 16), :].astype(F32)[8 * j : 8 * j + 8]
                both = jnp.concatenate([jnp.where(low, x, swap(y)), jnp.where(low, swap(x), y)], 0)
                both = pltpu.roll(both, lo, 1)
                put(t, jnp.where(take, both, last))
                last = both
            put(W // 128, jnp.where(take, 0.0, last))
        return carry

    lax.fori_loop(0, 4, pair, 0)
    own_ref[...] = acc_ref[0, : NC // 8, :].astype(BF16)
    other_ref[...] = acc_ref[1, : NC // 8, :].astype(BF16)


def merge_kernel(grad_ref, swapped_ref, *refs):
    out_ref = refs[-1]
    out_ref[: NC // 8, :] = swapped_ref[...]
    for start in range(0, W // 8, 64):
        total = grad_ref[start : start + 64, :].astype(F32)
        for j in range(1, 8):
            total += grad_ref[j * (W // 8) + start : j * (W // 8) + start + 64, :].astype(F32)
        out_ref[NC // 8 + start : NC // 8 + start + 64, :] = total.astype(BF16)


HOPS = (0, 1, -1, 2, -2, 3, -3, 4)


def finish_kernel(hops, *refs):
    n = len(hops)
    spec_ref, own, rest = refs[0], refs[1 : n + 1], refs[n + 1 : 2 * n + 1]
    new_ref, out_ref, sum_ref, turn_ref, sum_sem, turn_sem = refs[-6:]
    slab, led = lax.axis_index("slab"), lax.axis_index("led")
    upper = slab // 16
    copies = []
    for i, hop in enumerate(hops):
        source = lax.rem(led - hop + 8, 8)
        for part, half, ref in ((0, upper, own[i]), (1, 1 - upper, rest[i])):
            rows = pl.ds(pl.multiple_of(half * 64 + source * 8, 8), 8)
            for t in range(NC // 128):
                x = ref[t * 16 : t * 16 + 16, :].astype(F32)
                columns = slice(t * 128, t * 128 + 128)
                sum_ref[2 * i + part, 0, :, columns] = spec_ref[0, rows, columns] + x[:8]
                sum_ref[2 * i + part, 1, :, columns] = spec_ref[1, rows, columns] + x[8:]
            copies.append(
                pltpu.make_async_copy(sum_ref.at[2 * i + part], new_ref.at[:, rows, :], sum_sem.at[2 * i + part])
            )
            copies[-1].start()
        for t in range(2):
            start = NC // 8 + t * 128
            x = rest[i][start : start + 128, :].astype(F32).T
            turn_ref[i, 0, :, t * 128 : t * 128 + 128] = x[:BAND]
            turn_ref[i, 1, :, t * 128 : t * 128 + 128] = x[BAND:]
        columns = pl.ds(pl.multiple_of(source * 256, 256), 256)
        copies.append(pltpu.make_async_copy(turn_ref.at[i], out_ref.at[:, :, columns], turn_sem.at[i]))
        copies[-1].start()
    for copy in copies:
        copy.wait()


def finish(hops, spectrum, own, rest, before=()):
    n = len(hops)
    shapes = [jax.ShapeDtypeStruct((2, 128, NC), F32), jax.ShapeDtypeStruct((2, BAND, W), F32)]
    return pl.pallas_call(
        functools.partial(finish_kernel, hops),
        out_shape=shapes,
        in_specs=[pl.BlockSpec(memory_space=VMEM)] * (2 * n + 1) + [pl.BlockSpec(memory_space=pl.ANY)] * len(before),
        out_specs=[pl.BlockSpec(memory_space=pl.ANY)] * 2,
        input_output_aliases={2 * n + 1 + i: i for i in range(len(before))},
        scratch_shapes=[
            VMEM((2 * n, 2, 8, NC), F32),
            VMEM((n, 2, BAND, W // 8), F32),
            pltpu.SemaphoreType.DMA((2 * n,)),
            pltpu.SemaphoreType.DMA((n,)),
        ],
        compiler_params=pltpu.CompilerParams(vmem_limit_bytes=20 * MIB),
        cost_estimate=pl.CostEstimate(flops=0, bytes_accessed=n * 2 * MIB, transcendentals=0),
    )(spectrum, *own, *rest, *before)


def call(kernel, outs, scalars, arrays, scratch=(), flops=0, limit=20 * MIB):
    shapes = [jax.ShapeDtypeStruct(s, d) for s, d in outs]
    moved = sum(math.prod(s) * jnp.dtype(d).itemsize for s, d in outs)
    moved += sum(a.size * a.dtype.itemsize for a in arrays)
    return pl.pallas_call(
        kernel,
        out_shape=shapes,
        in_specs=[pl.BlockSpec(memory_space=pltpu.SMEM)] * len(scalars)
        + [pl.BlockSpec(memory_space=VMEM)] * len(arrays),
        out_specs=[pl.BlockSpec(memory_space=VMEM)] * len(outs),
        scratch_shapes=list(scratch),
        compiler_params=pltpu.CompilerParams(vmem_limit_bytes=limit),
        cost_estimate=pl.CostEstimate(flops=flops, bytes_accessed=moved, transcendentals=0),
    )(*scalars, *arrays)


def turn_bands(values):
    blocks = values.reshape(32, -1, 128)
    return lax.all_to_all(blocks, "slab", 0, 0).reshape(-1, 128)


FORWARD = [(i, (i + 1) % 8) for i in range(8)]
BACKWARD = [(i, (i - 1) % 8) for i in range(8)]


def ring_gather(piece, before=None):
    up = down = piece
    found = [piece]
    for hop in range(1, 5):
        if before is not None and hop == 2:
            up, down = lax.optimization_barrier((up, down, *before[3:5]))[:2]
        up = lax.ppermute(up, "led", FORWARD)
        found.append(up)
        if hop < 4:
            down = lax.ppermute(down, "led", BACKWARD)
            found.append(down)
    return found


def per_device(spectrum, pupil, intensity, row_offsets, col_offsets):
    base, turns = (jnp.asarray(x) for x in tables())
    rows128 = (W, 128)
    flops = 8 * QUARTER * 1024 * 128

    (outgoing,) = call(
        gather_kernel, [((2 * W, 128), BF16)], [col_offsets], [spectrum], [VMEM((2, 128, W + 128), BF16)]
    )
    arrived = turn_bands(outgoing)
    scratch = [VMEM(rows128, F32), VMEM((QUARTER, 512), F32)]
    first, window, pr, pi = call(
        first_kernel,
        [(rows128, BF16), (rows128, BF16), (rows128, F32), (rows128, F32)],
        [row_offsets],
        [arrived, pupil, base, turns],
        [VMEM((W + 16, 128), F32)] + scratch,
        flops,
    )
    turned = turn_bands(first)
    (second,) = call(
        middle_kernel, [(rows128, BF16)], [], [turned, intensity, base, turns], [VMEM(rows128, F32)] + scratch, 2 * flops
    )
    returned = turn_bands(second)
    gradient, correction = call(
        last_kernel,
        [(rows128, BF16), (rows128, BF16)],
        [row_offsets],
        [returned, window, pr, pi, base, turns],
        [VMEM(rows128, F32), VMEM((2 * W, 128), F32), VMEM((QUARTER, 512), F32)],
        flops,
    )
    landed = lax.all_to_all(correction.reshape(256, 8, 128), ("slab", "led"), 0, 0).reshape(rows128)
    gradient, landed = lax.optimization_barrier((gradient, landed))
    piece = NC // 8
    own, other = call(
        reduce_kernel,
        [((piece, 128), BF16)] * 2,
        [row_offsets, col_offsets],
        [landed],
        [VMEM((2, piece + 16, 128), F32)],
    )
    swapped = lax.ppermute(other, "slab", [(i, (i + 16) % 32) for i in range(32)])
    grads = lax.all_to_all(gradient.reshape(8, W // 8, 128), "led", 0, 0).reshape(rows128)
    own_pieces = ring_gather(own)
    (rest,) = call(merge_kernel, [((piece + W // 8, 128), BF16)], [], [grads, swapped, *own_pieces[1:3]])
    rest_pieces = ring_gather(rest, own_pieces)
    near = finish(HOPS[:7], spectrum, own_pieces[:7], rest_pieces[:7])
    return finish(HOPS[7:], spectrum, own_pieces[7:], rest_pieces[7:], near)


def solution(mesh):
    in_specs = (P(None, "slab", None), P(None, "slab", None), P("led", "slab", None), P(), P())
    out_specs = (P(None, "slab", None), P(None, "slab", None))
    return jax.shard_map(per_device, mesh=mesh, in_specs=in_specs, out_specs=out_specs, check_vma=False)
```
